32 devices in a mesh: groups: 2 (over x), row: 16 (over z, y, core).
Axes of the slice: x: 2, y: 2, z: 4, core: 2. Of those that a mesh axis runs over, the one named last changes fastest.
Arguments:
- atom_feat: bfloat16 [8192, 128], P(('groups', 'row')), parts along dimension 0, may hold values from -8 to 8
- window_start: int32 [256], P(('groups', 'row')), parts along dimension 0, may hold values from -64 to 4032, as said below
- atom_count: int32 [512], P(('groups', 'row')), parts along dimension 0, may hold values from 1 to 24, as said below
- residue_type: int32 [512], P(('groups', 'row')), parts along dimension 0, may hold values from 0 to 31
- chain_id: int32 [512], P(('groups', 'row')), parts along dimension 0, may hold values from 0 to 5, never falling along the last dimension, each value on 1 to 64 neighbouring positions
- token_single: bfloat16 [512, 768], P(('groups', 'row')), parts along dimension 0, may hold values from -6 to 6
- pair: bfloat16 [512, 256, 128], P(('groups', 'row')), parts along dimension 0, may hold values from -8 to 8
- atom_gain: float32 [128], replicated, may hold values from 0.25 to 1.75
- atom_qkv: bfloat16 [128, 384], replicated, may hold values from -1 to 1
- atom_out: bfloat16 [128, 128], replicated, may hold values from -0.5 to 0.5
- pool_weight: bfloat16 [128, 768], replicated, may hold values from -0.5 to 0.5
- restype_table: bfloat16 [32, 768], replicated, may hold values from -3 to 3
- token_gain: float32 [768], replicated, may hold values from 0.25 to 1.75
- token_proj: bfloat16 [768, 3072], replicated, may hold values from -0.21875 to 0.21875
- token_out: bfloat16 [768, 768], replicated, may hold values from -0.21875 to 0.21875
- pair_gain: float32 [128], replicated, may hold values from 0.1 to 1.9
- pair_bias_weight: bfloat16 [128, 16], replicated, may hold values from -16 to 16
- chain_weight: float32 [16], replicated, may hold values from -2 to 2
- back_weight: bfloat16 [768, 128], replicated, may hold values from -0.21875 to 0.21875
Outputs:
- atoms_out: bfloat16 [8192, 128], P(('groups', 'row')), parts along dimension 0
- tokens_out: bfloat16 [512, 768], P(('groups', 'row')), parts along dimension 0
The draws below stay inside these ranges and needn't reach their ends.
There are 2 independent parts, one for each index of `groups`. The reference program is written for one: setup_inputs(seed, part) draws one part's arguments, and reference() takes and returns one part's arrays. A program takes and returns all parts, laid end to end along the dimension named above; an argument that names none is the same for every part. Nothing has to cross between parts.
Inputs may be any that keep to these rules, and one draw needn't show every extreme that they name: `window_start`: key window b begins within 16 of b * 32 + 32 // 2 - 128 // 2. `atom_count`: atoms of token t follow those of token t - 1 and the counts sum to 4096; for every k, the first atom of token k * 16 lies within 64 of atom k * 256. `chain_id`: chain numbers never fall along the tokens.
All inputs are finite; a program needn't handle non-finite values.
Results may differ from the reference program's by a relative error of at most 0.008.
Values may be sent and summed in bfloat16 or wider, within the bound.
No kernel may reach another device: no remote copies, remote signals or barrier semaphores. Data moves between devices by JAX's collectives and lax.ppermute only.
A program may use at most 64 MiB of HBM per device.

```python
import math
import jax
import jax.numpy as jnp
import numpy as np
from jax import lax

CA = 128
CS = 768
CZ = 128
HEADS = 16
AHEADS = 4
RESTYPES = 32
QBLK = 32
KWIN = 128
JITTER = 16
MOSTA = 24
CHAINS = 6
ATOM_DEV = 256
TOK_DEV = 16
HDIM = 48
ADIM = 32
HALO = 64
DRIFT = 64
NA = 4096
NT = 256
NW = 128


def draw_window_start(key, part):
    blocks = jnp.arange(NA // QBLK, dtype=jnp.int32)
    jitters = jax.random.randint(key, (NA // QBLK,), -JITTER, JITTER + 1, dtype=jnp.int32)
    return blocks * QBLK + QBLK // 2 - KWIN // 2 + jitters


def draw_atom_count(key, part):
    key = jax.random.fold_in(key, 11)
    pick_key, drift_key, spot_key, weight_key, order_key = jax.random.split(key, 5)
    owners = NT // TOK_DEV
    top = MOSTA - 1
    chosen = jax.random.randint(pick_key, (), 1, owners - 1, dtype=jnp.int32)
    marks = jnp.arange(owners + 1, dtype=jnp.int32)
    offsets = jax.random.randint(drift_key, (owners + 1,), -DRIFT, DRIFT + 1, dtype=jnp.int32)
    offsets = jnp.where(marks == chosen, -DRIFT, offsets)
    offsets = jnp.where(marks == chosen + 1, DRIFT, offsets)
    offsets = jnp.where((marks == 0) | (marks == owners), 0, offsets)
    totals = ATOM_DEV + offsets[1:] - offsets[:-1]
    slots = jnp.arange(TOK_DEV, dtype=jnp.int32)
    spots = jax.random.randint(spot_key, (owners, 1), 0, TOK_DEV, dtype=jnp.int32)
    reserved = (marks[:owners, None] == chosen) & (slots[None, :] == spots)
    reserved_int = reserved.astype(jnp.int32)
    weights = jnp.where(reserved, 0, jax.random.randint(weight_key, (owners, TOK_DEV), 1, 5, dtype=jnp.int32))
    remain = totals - TOK_DEV - top * jnp.sum(reserved_int, axis=1)
    share = jnp.minimum(top, remain[:, None] * weights // jnp.sum(weights, axis=1, keepdims=True))
    room = jnp.where(reserved, 0, top - share)
    leftover = remain - jnp.sum(share, axis=1)
    ranking = jax.random.randint(order_key, (owners, TOK_DEV), 0, 1024, dtype=jnp.int32) * TOK_DEV + slots[None, :]
    order = jnp.argsort(ranking, axis=1)
    room_sorted = jnp.take_along_axis(room, order, axis=1)
    before = jnp.cumsum(room_sorted, axis=1) - room_sorted
    extra_sorted = jnp.clip(leftover[:, None] - before, 0, room_sorted)
    extra = jnp.take_along_axis(extra_sorted, jnp.argsort(order, axis=1), axis=1)
    counts = 1 + share + extra + top * reserved_int
    return counts.reshape(NT).astype(jnp.int32)


def draw_atom_feat(key, part):
    key = jax.random.fold_in(key, 12)
    first = jax.random.fold_in(key, 0)
    values = jnp.clip(jax.random.normal(first, (NA, CA), jnp.float32), -6.0, 6.0)
    return values.astype(jnp.bfloat16)


def draw_atom_qkv(key, part):
    key = jax.random.fold_in(key, 14)
    matrix = jnp.clip(jax.random.normal(key, (CA, 3 * CA), jnp.float32), -4.0, 4.0) / math.sqrt(CA)
    return matrix.astype(jnp.bfloat16)


def draw_pair(key, part):
    key = jax.random.fold_in(key, 13)
    first = jax.random.fold_in(key, 0)
    values = jnp.clip(jax.random.normal(first, (NT, NT, CZ), jnp.float32), -6.0, 6.0)
    return values.astype(jnp.bfloat16)


def draw_pair_bias_weight(key, part):
    key = jax.random.fold_in(key, 15)
    matrix = 2.0 * jnp.clip(jax.random.normal(key, (CZ, HEADS), jnp.float32), -4.0, 4.0) / math.sqrt(CZ)
    return matrix.astype(jnp.bfloat16)


def place_ends(drawn, key, least, largest):
    longest = drawn.shape.index(max(drawn.shape))
    spots = []
    for shift in (0, 1):
        where = [jax.random.randint(jax.random.fold_in(key, axis), (), 0, length) for axis, length in enumerate(drawn.shape)]
        where[longest] = (where[longest] + shift) % drawn.shape[longest]
        spots.append(tuple(where))
    return drawn.at[spots[0]].set(least).at[spots[1]].set(largest)


def shard_levels(stream_key, dims, pieces, smallest, high):
    loudness, own = 1.0, jax.random.fold_in(stream_key, 6)
    for dim, blocks in pieces:
        heights = jnp.exp(jax.random.uniform(jax.random.fold_in(own, dim), (blocks,), jnp.float32, smallest / len(pieces), high / len(pieces)))
        loudness = loudness * jnp.repeat(heights, dims[dim] // blocks).reshape([-1 if axis == dim else 1 for axis in range(len(dims))])
    return loudness


def profile(amount, total, most, lean):
    loads = [(1 << 20) // math.isqrt(standing ** lean) + 1 for standing in range(2, amount + 1)]
    spare, given = total - most - (amount - 1), [1] * (amount - 1)
    while spare > 0:
        candidates = [i for i in range(amount - 1) if given[i] < most]
        mass, remaining = sum([loads[i] for i in candidates]), spare
        for i in candidates:
            more = min(most - given[i], max(1, remaining * loads[i] // mass), spare)
            given[i] = given[i] + more
            spare = spare - more
    return np.array([most] + given)


def uneven(own_key, amount, total, limit, slope):
    if amount == 2:
        one = jax.random.randint(own_key, (), max(1, total - limit), min(limit, total - 1) + 1)
        return jnp.stack([one, total - one])
    sizes = jnp.asarray(profile(amount, total, limit, slope), jnp.int32)
    twos = (amount - 1) // 2
    giver, taker = sizes[1:1 + 2 * twos:2], sizes[2:2 + 2 * twos:2]
    margin = jnp.minimum(giver - 1, limit - taker)
    shifted = jax.random.randint(jax.random.fold_in(own_key, 1), (twos,), 0, 1 << 20) % (margin + 1)
    sizes = sizes.at[1:1 + 2 * twos:2].set(giver - shifted).at[2:2 + 2 * twos:2].set(taker + shifted)
    return sizes[jax.random.permutation(jax.random.fold_in(own_key, 2), amount)]


def centred(own_key, extent, deviation, limit, pieces=(), kind=jnp.bfloat16):
    array = deviation * jax.random.normal(own_key, extent, jnp.float32)
    if pieces:
        array = array * shard_levels(own_key, extent, pieces, -0.22, 0.18)
    return jnp.clip(array, -limit, limit).astype(kind)


def setup_inputs(seed: int = 0, part: int = 0) -> dict:
    key_of = jax.random.split(jax.random.key(seed), 20)
    part_keys = jax.random.split(jax.random.fold_in(key_of[19], part), 20)
    atom_feat = draw_atom_feat(jax.random.fold_in(jax.random.fold_in(key_of[19], part), 71), part)
    window_start = draw_window_start(jax.random.fold_in(jax.random.fold_in(key_of[19], part), 71), part)
    atom_count = draw_atom_count(jax.random.fold_in(jax.random.fold_in(key_of[19], part), 71), part)
    residue_type = place_ends(jax.random.randint(part_keys[3], (NT,), 0, RESTYPES), jax.random.fold_in(part_keys[3], 1), 0, RESTYPES - 1).astype(jnp.int32)
    chain_id = jnp.searchsorted(jnp.cumsum(uneven(part_keys[4], CHAINS, NT, NT // 4, 1)), jnp.arange(NT), side="right").astype(jnp.int32)
    token_single = centred(part_keys[5], (NT, CS), 1.0, 6.0, ((0, 16),))
    pair = draw_pair(jax.random.fold_in(jax.random.fold_in(key_of[19], part), 71), part)
    atom_gain = jnp.clip(1.0 + 0.15 * jax.random.normal(key_of[7], (CA,), jnp.float32), 0.25, 1.75)
    atom_qkv = draw_atom_qkv(jax.random.fold_in(key_of[19], 71), part)
    atom_out = centred(key_of[9], (CA, CA), CA ** -0.5, 0.5)
    pool_weight = centred(key_of[10], (CA, CS), CA ** -0.5, 0.5)
    restype_table = centred(key_of[11], (RESTYPES, CS), 0.5, 3.0)
    token_gain = jnp.clip(1.0 + 0.15 * jax.random.normal(key_of[12], (CS,), jnp.float32), 0.25, 1.75)
    token_proj = centred(key_of[13], (CS, 4 * CS), CS ** -0.5, 0.21875)
    token_out = centred(key_of[14], (CS, CS), CS ** -0.5, 0.21875)
    pair_gain = jnp.clip(1.0 + 0.18 * jax.random.normal(key_of[15], (CZ,), jnp.float32), 0.1, 1.9)
    pair_bias_weight = draw_pair_bias_weight(jax.random.fold_in(key_of[19], 71), part)
    chain_weight = jnp.clip(jax.random.uniform(key_of[17], (HEADS,), jnp.float32, -2.0, 2.0), -2.0, 2.0)
    back_weight = centred(key_of[18], (CS, CA), CS ** -0.5, 0.21875)
    return {"atom_feat": atom_feat, "window_start": window_start, "atom_count": atom_count, "residue_type": residue_type, "chain_id": chain_id, "token_single": token_single, "pair": pair, "atom_gain": atom_gain, "atom_qkv": atom_qkv, "atom_out": atom_out, "pool_weight": pool_weight, "restype_table": restype_table, "token_gain": token_gain, "token_proj": token_proj, "token_out": token_out, "pair_gain": pair_gain, "pair_bias_weight": pair_bias_weight, "chain_weight": chain_weight, "back_weight": back_weight}


def layer_norm(values, gain):
    centered = values - lax.optimization_barrier(jnp.mean(values, axis=-1, keepdims=True))
    variance = lax.optimization_barrier(jnp.mean(centered * centered, axis=-1, keepdims=True))
    return centered * lax.rsqrt(variance + 1e-05) * gain

def window_attend(queries, windows, inside):
    blocks = queries.shape[0]
    keys = windows[:, :, :CA].reshape(blocks, KWIN, AHEADS, ADIM).astype(jnp.float32)
    values = windows[:, :, CA:].reshape(blocks, KWIN, AHEADS, ADIM).astype(jnp.float32)
    scores = jnp.einsum('bqhd,bkhd->bhqk', queries.astype(jnp.float32), keys) / math.sqrt(ADIM)
    scores = jnp.where(inside[:, None, None, :], scores, -1000000000.0)
    weights = jnp.exp(scores - lax.optimization_barrier(jnp.max(scores, axis=-1, keepdims=True)))
    denom = lax.optimization_barrier(jnp.sum(weights, axis=-1, keepdims=True))
    mixed = jnp.einsum('bhqk,bkhd->bqhd', weights.astype(jnp.bfloat16).astype(jnp.float32), values)
    mixed = mixed / jnp.transpose(denom, (0, 2, 1, 3))
    return mixed.reshape(blocks * QBLK, CA).astype(jnp.bfloat16)

def reference(atom_feat, window_start, atom_count, residue_type, chain_id, token_single, pair, atom_gain, atom_qkv, atom_out, pool_weight, restype_table, token_gain, token_proj, token_out, pair_gain, pair_bias_weight, chain_weight, back_weight):
    ends = jnp.cumsum(atom_count).astype(jnp.int32)
    atom_token = jnp.searchsorted(ends, jnp.arange(NA, dtype=jnp.int32), side='right').astype(jnp.int32)
    normed = layer_norm(atom_feat.astype(jnp.float32), atom_gain).astype(jnp.bfloat16)
    atom_proj = jnp.dot(normed, atom_qkv, preferred_element_type=jnp.float32).astype(jnp.bfloat16)
    queries = atom_proj[:, :CA].reshape(NW, QBLK, AHEADS, ADIM)
    keyvals = jnp.pad(atom_proj[:, CA:], ((HALO, HALO), (0, 0)))
    anchors = (window_start + HALO).astype(jnp.int32)
    windows = jax.vmap(lambda anchor: lax.dynamic_slice_in_dim(keyvals, anchor, KWIN, 0))(anchors)
    position = window_start[:, None] + jnp.arange(KWIN, dtype=jnp.int32)[None, :]
    inside = (position >= 0) & (position < NA)
    attended = window_attend(queries, windows, inside)
    atoms_mid = (atom_feat.astype(jnp.float32) + jnp.dot(attended, atom_out, preferred_element_type=jnp.float32)).astype(jnp.bfloat16)
    lifted = jax.nn.relu(jnp.dot(atoms_mid, pool_weight, preferred_element_type=jnp.float32)).astype(jnp.bfloat16)
    pooled = jax.ops.segment_sum(lifted.astype(jnp.float32), atom_token, num_segments=NT)
    onehot = (residue_type[:, None] == jnp.arange(RESTYPES, dtype=jnp.int32)[None, :]).astype(jnp.bfloat16)
    state = token_single.astype(jnp.float32) + pooled / atom_count[:, None].astype(jnp.float32)
    state = state + jnp.dot(onehot, restype_table, preferred_element_type=jnp.float32)
    token_normed = layer_norm(state, token_gain).astype(jnp.bfloat16)
    token_all = jnp.dot(token_normed, token_proj, preferred_element_type=jnp.float32)
    qkv_part = token_all[:, :3 * CS].astype(jnp.bfloat16).astype(jnp.float32)
    query = qkv_part[:, :CS].reshape(NT, HEADS, HDIM)
    keys = qkv_part[:, CS:2 * CS].reshape(NT, HEADS, HDIM)
    values = qkv_part[:, 2 * CS:].reshape(NT, HEADS, HDIM)
    gate = jax.nn.sigmoid(token_all[:, 3 * CS:])

    def pair_bias(rows):
        pair_normed = layer_norm(rows.astype(jnp.float32), pair_gain).astype(jnp.bfloat16)
        return jnp.einsum('tkc,ch->thk', pair_normed.astype(jnp.float32), pair_bias_weight.astype(jnp.float32))
    bias = lax.map(pair_bias, pair.reshape(NT // TOK_DEV, TOK_DEV, NT, CZ)).reshape(NT, HEADS, NT)
    same = (chain_id[:, None] == chain_id[None, :]).astype(jnp.float32)
    scores = jnp.einsum('thd,khd->thk', query, keys) / math.sqrt(HDIM) + bias
    scores = scores + chain_weight[None, :, None] * same[:, None, :]
    weights = jnp.exp(scores - lax.optimization_barrier(jnp.max(scores, axis=-1, keepdims=True)))
    denom = lax.optimization_barrier(jnp.sum(weights, axis=-1))
    mixed = jnp.einsum('thk,khd->thd', weights.astype(jnp.bfloat16).astype(jnp.float32), values) / denom[:, :, None]
    gated = (mixed.reshape(NT, CS) * gate).astype(jnp.bfloat16)
    tokens_out = (state + jnp.dot(gated, token_out, preferred_element_type=jnp.float32)).astype(jnp.bfloat16)
    back = jnp.dot(tokens_out, back_weight, preferred_element_type=jnp.float32).astype(jnp.bfloat16)
    atoms_out = (atoms_mid.astype(jnp.float32) + back[atom_token].astype(jnp.float32)).astype(jnp.bfloat16)
    return (atoms_out, tokens_out)
```

```python
import functools
import math

import jax
import jax.numpy as jnp
from jax import lax
from jax.experimental import pallas as pl
from jax.experimental.pallas import tpu as pltpu
from jax.sharding import PartitionSpec as P

CA = 128
CS = 768
HEADS = 16
AHEADS = 4
RESTYPES = 32
QBLK = 32
KWIN = 128
HDIM = 48
ADIM = 32
HALF = 128
REACH = 64
EPS = 1e-05
NEG = -1e30
F32 = jnp.float32
BF16 = jnp.bfloat16
VMEM_LIMIT = 24 * 1024 * 1024

COUNT, CHAIN, RES, WIN = 0, 16, 32, 48
TABLE = 128


def dot(a, b):
    return lax.dot_general(a, b, (((1,), (0,)), ((), ())), preferred_element_type=F32)


def dot_nt(a, b):
    return lax.dot_general(a, b, (((1,), (1,)), ((), ())), preferred_element_type=F32)


def norm(x, gain):
    centered = x - jnp.mean(x, axis=-1, keepdims=True)
    variance = jnp.mean(centered * centered, axis=-1, keepdims=True)
    return centered * lax.rsqrt(variance + EPS) * gain


def iota(shape, axis):
    return lax.broadcasted_iota(jnp.int32, shape, axis)


def table_row(table, row):
    return jnp.sum(jnp.where(iota(table.shape, 0) == row, table, 0), axis=0, keepdims=True)


def column(row, base, size):
    shape = (size, row.shape[1])
    return jnp.sum(jnp.where(iota(shape, 1) == iota(shape, 0) + base, row, 0), axis=1, keepdims=True)


def atoms_before(table, row, tokens):
    keep = (iota(table.shape, 0) < row) & (iota(table.shape, 1) < COUNT + tokens)
    return jnp.sum(jnp.sum(jnp.where(keep, table, 0), axis=0, keepdims=True), axis=1, keepdims=True)


def pair_kernel(pair_ref, gain_ref, weight_ref, bias_ref):
    gain, weight = gain_ref[...], weight_ref[...]
    for t in range(pair_ref.shape[0]):
        normed = norm(pair_ref[t].astype(F32), gain).astype(BF16)
        bias_ref[t * HEADS : (t + 1) * HEADS, :] = dot_nt(weight, normed)


def atom_kernel(
    n,
    feat_ref,
    core_ref,
    far_ref,
    table_ref,
    single_ref,
    gain_ref,
    qkv_ref,
    out_ref,
    pool_ref,
    restype_ref,
    token_gain_ref,
    mid_ref,
    state_ref,
    normed_ref,
):
    me = lax.axis_index("row")
    even = lax.rem(me, 2) == 0
    rows = feat_ref.shape[0]
    tokens = single_ref.shape[0]
    table = table_ref[...]
    own_row = table_row(table, me)
    left = jnp.where(even, far_ref[rows - HALF :, :], core_ref[rows - HALF :, :])
    right = jnp.where(even, core_ref[:HALF, :], far_ref[:HALF, :])
    feat = jnp.concatenate([left, feat_ref[...], right], axis=0)
    normed = norm(feat.astype(F32), gain_ref[...]).astype(BF16)
    proj = dot(normed, qkv_ref[...]).astype(BF16)
    span = rows + 2 * REACH
    windows = rows // QBLK
    edge = REACH // QBLK
    win_left = table_row(table, me - 1)
    win_right = table_row(table, me + 1)
    mids = []
    for s in range(span // HALF):
        begin = REACH + HALF * s
        queries = proj[begin : begin + HALF, :CA]
        keys = proj[HALF * s : HALF * s + 2 * HALF, CA : 2 * CA]
        values = proj[HALF * s : HALF * s + 2 * HALF, 2 * CA :]
        head = iota((HALF, CA), 1) // ADIM
        stacked = jnp.concatenate(
            [jnp.where(head == h, queries, jnp.zeros_like(queries)) for h in range(AHEADS)], axis=0
        )
        scores = dot_nt(stacked, keys) * (1.0 / math.sqrt(ADIM))
        shape = (HALF, TABLE)
        block = iota(shape, 0) // QBLK + (HALF // QBLK) * s - edge
        lane = iota(shape, 1) - WIN
        begins = jnp.where((block >= 0) & (block < windows) & (lane == block), own_row, 0)
        if s == 0:
            begins += jnp.where((block < 0) & (lane == block + windows), win_left, 0)
        if s == span // HALF - 1:
            begins += jnp.where((block >= windows) & (lane == block - windows), win_right, 0)
        start = jnp.sum(begins, axis=1, keepdims=True)
        shape = (HALF, 2 * HALF)
        place = iota(shape, 1) + (me * rows - HALF + HALF * s)
        inside = (place >= start) & (place < start + KWIN) & (place >= 0) & (place < n * rows)
        inside = jnp.concatenate([inside.astype(F32)] * AHEADS, axis=0) > 0.5
        scores = jnp.where(inside, scores, NEG)
        weights = jnp.exp(scores - jnp.max(scores, axis=-1, keepdims=True))
        denom = jnp.sum(weights, axis=-1, keepdims=True)
        mixed = dot(weights.astype(BF16), values) / denom
        total = jnp.zeros((HALF, CA), F32)
        for h in range(AHEADS):
            total = total + jnp.where(head == h, mixed[h * HALF : (h + 1) * HALF], 0.0)
        added = dot(total.astype(BF16), out_ref[...])
        mids.append((feat[begin : begin + HALF].astype(F32) + added).astype(BF16))
    mid = jnp.concatenate(mids, axis=0)
    mid_ref[...] = mid[REACH : REACH + rows]
    lifted = jnp.maximum(dot(mid, pool_ref[...]), 0.0).astype(BF16)
    count = column(own_row, COUNT, tokens)
    shape = (tokens, TABLE)
    ahead = (iota(shape, 1) >= COUNT) & (iota(shape, 1) < COUNT + iota(shape, 0))
    begin = atoms_before(table, me, tokens) + jnp.sum(
        jnp.where(ahead, own_row, 0), axis=1, keepdims=True
    )
    atom = iota((tokens, span), 1) + (me * rows - REACH)
    chosen = (atom >= begin) & (atom < begin + count)
    pooled = dot(jnp.where(chosen, 1.0, 0.0).astype(BF16), lifted)
    kind = column(own_row, RES, tokens)
    onehot = jnp.where(iota((tokens, RESTYPES), 1) == kind, 1.0, 0.0).astype(BF16)
    state = single_ref[...].astype(F32) + pooled / count.astype(F32)
    state = state + dot(onehot, restype_ref[...])
    state_ref[...] = state
    token_normed = norm(state, token_gain_ref[...]).astype(BF16)
    for i in range(normed_ref.shape[0]):
        normed_ref[i] = token_normed


def query_kernel(
    normed_ref, table_ref, bias_ref, chain_weight_ref, wq_ref, wk_ref, wg_ref,
    query_ref, gate_ref, biased_ref, before_ref, own_ref, after_ref,
):
    me = lax.axis_index("row")
    normed = normed_ref[0]
    tokens = normed.shape[0]
    query = dot(normed, wq_ref[...]).astype(BF16)
    gate_ref[...] = jax.nn.sigmoid(dot(normed, wg_ref[...]))
    head = iota((HEADS, CS), 1) // HDIM == iota((HEADS, CS), 0)
    spread = jnp.concatenate(
        [
            jnp.where(head, jnp.broadcast_to(query[t : t + 1].astype(F32), (HEADS, CS)), 0.0)
            for t in range(tokens)
        ],
        axis=0,
    ).astype(BF16)
    query_ref[...] = dot_nt(spread, wk_ref[...]).astype(BF16)
    table = table_ref[...]
    n = table.shape[0]
    keys = n * tokens
    shape = (TABLE, keys)
    pick = jnp.where(iota(shape, 0) == CHAIN + iota(shape, 1) % tokens, 1.0, 0.0).astype(BF16)
    each = dot(table.astype(F32).astype(BF16), pick)
    shape = (n, keys)
    chain_keys = jnp.sum(
        jnp.where(iota(shape, 1) // tokens == iota(shape, 0), each, 0.0), axis=0, keepdims=True
    )
    own_row = table_row(table, me)
    shape = (tokens * HEADS, TABLE)
    mine = iota(shape, 1) == CHAIN + iota(shape, 0) // HEADS
    chain_rows = jnp.sum(jnp.where(mine, own_row, 0), axis=1, keepdims=True).astype(F32)
    shape = (tokens * HEADS, HEADS)
    mine = iota(shape, 1) == iota(shape, 0) % HEADS
    weight = jnp.sum(jnp.where(mine, chain_weight_ref[...], 0.0), axis=1, keepdims=True)
    biased_ref[...] = bias_ref[...] + jnp.where(chain_rows == chain_keys, weight, 0.0)
    rows = own_ref.shape[0]
    counts = jnp.where(iota(table.shape, 1) < COUNT + tokens, table, 0).astype(F32)
    shape = (TABLE, tokens)
    ahead = jnp.where(iota(shape, 0) < COUNT + iota(shape, 1), 1.0, 0.0).astype(BF16)
    starts = dot(counts.astype(BF16), ahead)
    atom = (iota((rows, tokens), 0) + me * rows).astype(F32)
    for step, ref in ((-1, before_ref), (0, own_ref), (1, after_ref)):
        at = iota(starts.shape, 0) == me + step
        begin = jnp.sum(jnp.where(at, starts, 0.0), axis=0, keepdims=True)
        begin = begin + atoms_before(table, me + step, tokens).astype(F32)
        size = jnp.sum(jnp.where(at, counts[:, COUNT : COUNT + tokens], 0.0), axis=0, keepdims=True)
        ref[...] = jnp.where((atom >= begin) & (atom < begin + size), 1.0, 0.0).astype(BF16)


def attend_kernel(
    mine_ref, other_ref, query_ref, biased_ref, gate_ref, state_ref, wv_ref, out_ref, back_ref,
    tokens_ref, result_ref,
):
    even = lax.rem(lax.axis_index("row"), 2) == 0
    tokens = state_ref.shape[0]
    chips = mine_ref.shape[0]
    mine, other = mine_ref[...], other_ref[...]
    first = jnp.where(even, mine, other)
    second = jnp.where(even, other, mine)
    normed = jnp.concatenate(
        [part[c] for c in range(chips) for part in (first, second)], axis=0
    )
    scores = dot_nt(query_ref[...], normed) * (1.0 / math.sqrt(HDIM)) + biased_ref[...]
    values = dot(normed, wv_ref[...]).astype(BF16)
    weights = jnp.exp(scores - jnp.max(scores, axis=-1, keepdims=True))
    denom = jnp.sum(weights, axis=-1, keepdims=True)
    mixed = dot(weights.astype(BF16), values) / denom
    head = iota((HEADS, CS), 1) // HDIM == iota((HEADS, CS), 0)
    mixed = jnp.concatenate(
        [
            jnp.sum(
                jnp.where(head, mixed[t * HEADS : (t + 1) * HEADS], 0.0), axis=0, keepdims=True
            )
            for t in range(tokens)
        ],
        axis=0,
    )
    gated = (mixed * gate_ref[...]).astype(BF16)
    updated = (state_ref[...] + dot(gated, out_ref[...])).astype(BF16)
    tokens_ref[...] = updated
    result_ref[...] = dot(updated, back_ref[...]).astype(BF16)


def spread_kernel(mid_ref, back_ref, core_ref, far_ref, before_ref, own_ref, after_ref, atoms_ref):
    even = lax.rem(lax.axis_index("row"), 2) == 0
    core, far = core_ref[...], far_ref[...]
    total = dot(before_ref[...], jnp.where(even, far, core))
    total = total + dot(own_ref[...], back_ref[...])
    total = total + dot(after_ref[...], jnp.where(even, core, far))
    atoms_ref[...] = (mid_ref[...].astype(F32) + total).astype(BF16)


def call(kernel, outs, *args):
    return pl.pallas_call(
        kernel,
        out_shape=outs,
        in_specs=[pl.BlockSpec(memory_space=pltpu.VMEM)] * len(args),
        out_specs=jax.tree.map(lambda _: pl.BlockSpec(memory_space=pltpu.VMEM), outs),
        compiler_params=pltpu.CompilerParams(vmem_limit_bytes=VMEM_LIMIT),
    )(*args)


def shape_of(shape, dtype):
    return jax.ShapeDtypeStruct(shape, dtype)


def shards(
    atom_feat,
    window_start,
    atom_count,
    residue_type,
    chain_id,
    token_single,
    pair,
    atom_gain,
    atom_qkv,
    atom_out,
    pool_weight,
    restype_table,
    token_gain,
    token_proj,
    token_out,
    pair_gain,
    pair_bias_weight,
    chain_weight,
    back_weight,
):
    n = lax.axis_size("row")
    rows, tokens, extent = atom_feat.shape[0], token_single.shape[0], pair.shape[1]
    cores = [(i, i ^ 1) for i in range(n)]
    far = [(i, i + 1) for i in range(1, n - 1, 2)] + [(i + 1, i) for i in range(1, n - 1, 2)]
    same_core = [[2 * c + core for c in range(n // 2)] for core in range(2)]

    feat_far = lax.ppermute(atom_feat, "row", far)
    feat_core = lax.ppermute(atom_feat, "row", cores)
    ints = jnp.concatenate([atom_count, chain_id, residue_type, window_start])
    ints = jnp.pad(ints, (0, TABLE - ints.shape[0]))
    table = lax.all_to_all(jnp.broadcast_to(ints[None], (n, TABLE)), "row", 0, 0, tiled=True)

    bias = call(
        pair_kernel,
        shape_of((tokens * HEADS, extent), F32),
        pair,
        pair_gain[None],
        pair_bias_weight.T,
    )
    mid, state, normed = call(
        functools.partial(atom_kernel, n),
        (
            shape_of((rows, CA), BF16),
            shape_of((tokens, CS), F32),
            shape_of((n // 2, tokens, CS), BF16),
        ),
        atom_feat,
        feat_core,
        feat_far,
        table,
        token_single,
        atom_gain[None],
        atom_qkv,
        atom_out,
        pool_weight,
        restype_table,
        token_gain[None],
    )
    mine = lax.all_to_all(normed, "row", 0, 0, tiled=True, axis_index_groups=same_core)
    other = lax.ppermute(mine, "row", cores)
    pick = shape_of((rows, tokens), BF16)
    query, gate, biased, before, own, after = call(
        query_kernel,
        (
            shape_of((tokens * HEADS, CS), BF16),
            shape_of((tokens, CS), F32),
            shape_of((tokens * HEADS, extent), F32),
            pick,
            pick,
            pick,
        ),
        normed,
        table,
        bias,
        chain_weight[None],
        token_proj[:, :CS],
        token_proj[:, CS : 2 * CS],
        token_proj[:, 3 * CS :],
    )
    tokens_out, back = call(
        attend_kernel,
        (shape_of((tokens, CS), BF16), shape_of((tokens, CA), BF16)),
        mine,
        other,
        query,
        biased,
        gate,
        state,
        token_proj[:, 2 * CS : 3 * CS],
        token_out,
        back_weight,
    )
    back_far = lax.ppermute(back, "row", far)
    back_core = lax.ppermute(back, "row", cores)
    atoms_out = call(
        spread_kernel, shape_of((rows, CA), BF16),
        mid, back, back_core, back_far, before, own, after,
    )
    return (atoms_out, tokens_out)


def solution(mesh):
    split = P(("groups", "row"), None)
    line = P(("groups", "row"))
    return jax.shard_map(
        shards,
        mesh=mesh,
        in_specs=(split, line, line, line, line, split, P(("groups", "row"), None, None))
        + (P(),) * 12,
        out_specs=(split, split),
        check_vma=False,
    )
```

```python
import functools
import math

import jax
import jax.numpy as jnp
from jax import lax
from jax.experimental import pallas as pl
from jax.experimental.pallas import tpu as pltpu
from jax.sharding import PartitionSpec as P

CA = 128
CS = 768
HEADS = 16
AHEADS = 4
RESTYPES = 32
QBLK = 32
KWIN = 128
HDIM = 48
ADIM = 32
HALF = 128
REACH = 64
COST = 2_000_000_000
EPS = 1e-05
NEG = -1e30
F32 = jnp.float32
BF16 = jnp.bfloat16
COUNT, CHAIN, RES, WIN = 0, 16, 32, 48
TABLE = 128


def dot(a, b):
    return lax.dot_general(a, b, (((1,), (0,)), ((), ())), preferred_element_type=F32)


def dot_nt(a, b):
    return lax.dot_general(a, b, (((1,), (1,)), ((), ())), preferred_element_type=F32)


def norm(x, gain):
    centered = x - jnp.mean(x, axis=-1, keepdims=True)
    variance = jnp.mean(centered * centered, axis=-1, keepdims=True)
    return centered * lax.rsqrt(variance + EPS) * gain


def iota(shape, axis):
    return lax.broadcasted_iota(jnp.int32, shape, axis)


def table_row(table, row):
    return jnp.sum(jnp.where(iota(table.shape, 0) == row, table, 0), axis=0, keepdims=True)


def column(row, base, size):
    shape = (size, row.shape[1])
    return jnp.sum(jnp.where(iota(shape, 1) == iota(shape, 0) + base, row, 0), axis=1, keepdims=True)


def atoms_before(table, row, tokens):
    keep = (iota(table.shape, 0) < row) & (iota(table.shape, 1) < COUNT + tokens)
    return jnp.sum(jnp.sum(jnp.where(keep, table, 0), axis=0, keepdims=True), axis=1, keepdims=True)


def table_kernel(row_ref, table_ref):
    table_ref[...] = jnp.broadcast_to(row_ref[...][None], table_ref.shape)


def pair_kernel(pair_ref, gain_ref, weight_ref, bias_ref):
    gain, weight = gain_ref[...], weight_ref[...]
    for t in range(pair_ref.shape[0]):
        normed = norm(pair_ref[t].astype(F32), gain).astype(BF16)
        bias_ref[t * HEADS : (t + 1) * HEADS, :] = dot_nt(weight, normed)


def atom_kernel(
    n,
    feat_ref,
    core_ref,
    far_ref,
    table_ref,
    single_ref,
    gain_ref,
    qkv_ref,
    out_ref,
    pool_ref,
    restype_ref,
    token_gain_ref,
    bias_ref,
    mid_ref,
    state_ref,
    normed_ref,
):
    me = lax.axis_index("row")
    even = lax.rem(me, 2) == 0
    rows = feat_ref.shape[0]
    tokens = single_ref.shape[0]
    table = table_ref[...]
    own_row = table_row(table, me)
    left = jnp.where(even, far_ref[rows - HALF :, :], core_ref[rows - HALF :, :])
    right = jnp.where(even, core_ref[:HALF, :], far_ref[:HALF, :])
    feat = jnp.concatenate([left, feat_ref[...], right], axis=0)
    normed = norm(feat.astype(F32), gain_ref[...]).astype(BF16)
    proj = dot(normed, qkv_ref[...]).astype(BF16)
    span = rows + 2 * REACH
    windows = rows // QBLK
    edge = REACH // QBLK
    win_left = table_row(table, me - 1)
    win_right = table_row(table, me + 1)
    mids = []
    for s in range(span // HALF):
        begin = REACH + HALF * s
        queries = proj[begin : begin + HALF, :CA]
        keys = proj[HALF * s : HALF * s + 2 * HALF, CA : 2 * CA]
        values = proj[HALF * s : HALF * s + 2 * HALF, 2 * CA :]
        head = iota((HALF, CA), 1) // ADIM
        stacked = jnp.concatenate(
            [jnp.where(head == h, queries, jnp.zeros_like(queries)) for h in range(AHEADS)], axis=0
        )
        scores = dot_nt(stacked, keys) * (1.0 / math.sqrt(ADIM))
        shape = (HALF, TABLE)
        block = iota(shape, 0) // QBLK + (HALF // QBLK) * s - edge
        lane = iota(shape, 1) - WIN
        begins = jnp.where((block >= 0) & (block < windows) & (lane == block), own_row, 0)
        if s == 0:
            begins += jnp.where((block < 0) & (lane == block + windows), win_left, 0)
        if s == span // HALF - 1:
            begins += jnp.where((block >= windows) & (lane == block - windows), win_right, 0)
        start = jnp.sum(begins, axis=1, keepdims=True)
        shape = (HALF, 2 * HALF)
        place = iota(shape, 1) + (me * rows - HALF + HALF * s)
        inside = (place >= start) & (place < start + KWIN) & (place >= 0) & (place < n * rows)
        inside = jnp.concatenate([inside.astype(F32)] * AHEADS, axis=0) > 0.5
        scores = jnp.where(inside, scores, NEG)
        weights = jnp.exp(scores - jnp.max(scores, axis=-1, keepdims=True))
        denom = jnp.sum(weights, axis=-1, keepdims=True)
        mixed = dot(weights.astype(BF16), values) / denom
        total = jnp.zeros((HALF, CA), F32)
        for h in range(AHEADS):
            total = total + jnp.where(head == h, mixed[h * HALF : (h + 1) * HALF], 0.0)
        added = dot(total.astype(BF16), out_ref[...])
        mids.append((feat[begin : begin + HALF].astype(F32) + added).astype(BF16))
    mid = jnp.concatenate(mids, axis=0)
    mid_ref[...] = mid[REACH : REACH + rows]
    lifted = jnp.maximum(dot(mid, pool_ref[...]), 0.0).astype(BF16)
    count = column(own_row, COUNT, tokens)
    shape = (tokens, TABLE)
    ahead = (iota(shape, 1) >= COUNT) & (iota(shape, 1) < COUNT + iota(shape, 0))
    begin = atoms_before(table, me, tokens) + jnp.sum(
        jnp.where(ahead, own_row, 0), axis=1, keepdims=True
    )
    atom = iota((tokens, span), 1) + (me * rows - REACH)
    chosen = (atom >= begin) & (atom < begin + count)
    pooled = dot(jnp.where(chosen, 1.0, 0.0).astype(BF16), lifted)
    kind = column(own_row, RES, tokens)
    onehot = jnp.where(iota((tokens, RESTYPES), 1) == kind, 1.0, 0.0).astype(BF16)
    state = single_ref[...].astype(F32) + pooled / count.astype(F32)
    state = state + dot(onehot, restype_ref[...])
    state_ref[...] = state
    token_normed = norm(state, token_gain_ref[...]).astype(BF16)
    for i in range(normed_ref.shape[0]):
        normed_ref[i] = token_normed


def query_kernel(
    normed_ref, table_ref, bias_ref, chain_weight_ref, proj_ref,
    query_ref, gate_ref, biased_ref, pick_ref,
):
    me = lax.axis_index("row")
    normed = normed_ref[0]
    tokens = normed.shape[0]
    query = dot(normed, proj_ref[:, :CS]).astype(BF16)
    head = iota((HEADS, CS), 1) // HDIM == iota((HEADS, CS), 0)
    spread = jnp.concatenate(
        [
            jnp.where(head, jnp.broadcast_to(query[t : t + 1].astype(F32), (HEADS, CS)), 0.0)
            for t in range(tokens)
        ],
        axis=0,
    ).astype(BF16)
    query_ref[...] = dot_nt(spread, proj_ref[:, CS : 2 * CS]).astype(BF16)
    table = table_ref[...]
    n = table.shape[0]
    keys = n * tokens
    shape = (TABLE, keys)
    pick = jnp.where(iota(shape, 0) == CHAIN + iota(shape, 1) % tokens, 1.0, 0.0).astype(BF16)
    each = dot(table.astype(F32).astype(BF16), pick)
    shape = (n, keys)
    chain_keys = jnp.sum(
        jnp.where(iota(shape, 1) // tokens == iota(shape, 0), each, 0.0), axis=0, keepdims=True
    )
    own_row = table_row(table, me)
    shape = (tokens * HEADS, TABLE)
    mine = iota(shape, 1) == CHAIN + iota(shape, 0) // HEADS
    chain_rows = jnp.sum(jnp.where(mine, own_row, 0), axis=1, keepdims=True).astype(F32)
    shape = (tokens * HEADS, HEADS)
    mine = iota(shape, 1) == iota(shape, 0) % HEADS
    weight = jnp.sum(jnp.where(mine, chain_weight_ref[...], 0.0), axis=1, keepdims=True)
    biased_ref[...] = bias_ref[...] + jnp.where(chain_rows == chain_keys, weight, 0.0)
    rows = pick_ref.shape[0]
    counts = jnp.where(iota(table.shape, 1) < COUNT + tokens, table, 0).astype(F32).astype(BF16)
    begin = jnp.zeros((1, TABLE), F32)
    size = jnp.zeros((1, TABLE), F32)
    for step in range(3):
        shape = (TABLE, TABLE)
        token = iota(shape, 1) - step * tokens
        here = (token >= 0) & (token < tokens)
        ahead = jnp.where(here & (iota(shape, 0) < COUNT + token), 1.0, 0.0).astype(BF16)
        equal = jnp.where(here & (iota(shape, 0) == COUNT + token), 1.0, 0.0).astype(BF16)
        at = iota(table.shape, 0) == me + step - 1
        begin += jnp.sum(jnp.where(at, dot(counts, ahead), 0.0), axis=0, keepdims=True)
        size += jnp.sum(jnp.where(at, dot(counts, equal), 0.0), axis=0, keepdims=True)
        before = atoms_before(table, me + step - 1, tokens).astype(F32)
        begin += jnp.where(here[:1], before, 0.0)
    atom = (iota((rows, TABLE), 0) + me * rows).astype(F32)
    pick_ref[...] = jnp.where((atom >= begin) & (atom < begin + size), 1.0, 0.0).astype(BF16)
    gate_ref[...] = jax.nn.sigmoid(dot(normed, proj_ref[:, 3 * CS :]))


def attend_kernel(
    mine_ref, other_ref, query_ref, biased_ref, gate_ref, state_ref, out_ref, back_ref, proj_ref,
    tokens_ref, result_ref,
    wv_ref, sem,
):
    copy = pltpu.make_async_copy(proj_ref.at[:, pl.ds(2 * CS, CS)], wv_ref, sem)
    copy.start()
    even = lax.rem(lax.axis_index("row"), 2) == 0
    tokens = state_ref.shape[0]
    chips = mine_ref.shape[0]
    mine, other = mine_ref[...], other_ref[...]
    first = jnp.where(even, mine, other)
    second = jnp.where(even, other, mine)
    normed = jnp.concatenate(
        [part[c] for c in range(chips) for part in (first, second)], axis=0
    )
    scores = dot_nt(query_ref[...], normed) * (1.0 / math.sqrt(HDIM)) + biased_ref[...]
    weights = jnp.exp(scores - jnp.max(scores, axis=-1, keepdims=True))
    denom = jnp.sum(weights, axis=-1, keepdims=True)
    copy.wait()
    values = dot(normed, wv_ref[...]).astype(BF16)
    mixed = dot(weights.astype(BF16), values) / denom
    head = iota((HEADS, CS), 1) // HDIM == iota((HEADS, CS), 0)
    mixed = jnp.concatenate(
        [
            jnp.sum(
                jnp.where(head, mixed[t * HEADS : (t + 1) * HEADS], 0.0), axis=0, keepdims=True
            )
            for t in range(tokens)
        ],
        axis=0,
    )
    gated = (mixed * gate_ref[...]).astype(BF16)
    updated = (state_ref[...] + dot(gated, out_ref[...])).astype(BF16)
    tokens_ref[...] = updated
    result_ref[...] = dot(updated, back_ref[...]).astype(BF16)


def spread_kernel(mid_ref, back_ref, core_ref, far_ref, pick_ref, atoms_ref):
    even = lax.rem(lax.axis_index("row"), 2) == 0
    core, far, own = core_ref[...], far_ref[...], back_ref[...]
    rest = jnp.zeros((TABLE - 3 * own.shape[0], CA), BF16)
    parts = [jnp.where(even, far, core), own, jnp.where(even, core, far), rest]
    spread = dot(pick_ref[...], jnp.concatenate(parts, axis=0))
    atoms_ref[...] = (mid_ref[...].astype(F32) + spread).astype(BF16)


def call(kernel, outs, *args, hbm=(), limit=24, scratch=()):
    spec = pl.BlockSpec(memory_space=pltpu.VMEM)
    return pl.pallas_call(
        kernel,
        out_shape=outs,
        in_specs=[spec] * len(args) + [pl.BlockSpec(memory_space=pltpu.HBM)] * len(hbm),
        out_specs=jax.tree.map(lambda _: spec, outs),
        scratch_shapes=list(scratch),
        compiler_params=pltpu.CompilerParams(vmem_limit_bytes=limit * 1024 * 1024),
        cost_estimate=pl.CostEstimate(flops=COST, bytes_accessed=COST // 200, transcendentals=0),
    )(*args, *hbm)


def shape_of(shape, dtype):
    return jax.ShapeDtypeStruct(shape, dtype)


def shards(
    atom_feat,
    window_start,
    atom_count,
    residue_type,
    chain_id,
    token_single,
    pair,
    atom_gain,
    atom_qkv,
    atom_out,
    pool_weight,
    restype_table,
    token_gain,
    token_proj,
    token_out,
    pair_gain,
    pair_bias_weight,
    chain_weight,
    back_weight,
):
    n = lax.axis_size("row")
    rows, tokens, extent = atom_feat.shape[0], token_single.shape[0], pair.shape[1]
    cores = [(i, i ^ 1) for i in range(n)]
    far = [(i, i + 1) for i in range(1, n - 1, 2)] + [(i + 1, i) for i in range(1, n - 1, 2)]
    same_core = [[2 * c + core for c in range(n // 2)] for core in range(2)]

    feat_far = lax.ppermute(atom_feat, "row", far)
    feat_core = lax.ppermute(atom_feat, "row", cores)
    ints = jnp.concatenate([atom_count, chain_id, residue_type, window_start])
    ints = jnp.pad(ints, (0, TABLE - ints.shape[0]))[None]
    table = call(table_kernel, shape_of((n, 1, TABLE), jnp.int32), ints)
    table = lax.all_to_all(table, "row", 0, 0, tiled=True).reshape(n, TABLE)

    bias = call(
        pair_kernel, shape_of((tokens * HEADS, extent), F32), pair, pair_gain, pair_bias_weight.T
    )
    mid, state, normed = call(
        functools.partial(atom_kernel, n),
        (
            shape_of((rows, CA), BF16),
            shape_of((tokens, CS), F32),
            shape_of((n // 2, tokens, CS), BF16),
        ),
        atom_feat,
        feat_core,
        feat_far,
        table,
        token_single,
        atom_gain,
        atom_qkv,
        atom_out,
        pool_weight,
        restype_table,
        token_gain,
        bias,
    )
    mine = lax.all_to_all(normed, "row", 0, 0, tiled=True, axis_index_groups=same_core)
    query, gate, biased, pick = call(
        query_kernel,
        (
            shape_of((tokens * HEADS, CS), BF16),
            shape_of((tokens, CS), F32),
            shape_of((tokens * HEADS, extent), F32),
            shape_of((rows, TABLE), BF16),
        ),
        normed,
        table,
        bias,
        chain_weight,
        token_proj,
    )
    mine, query = lax.optimization_barrier((mine, query))
    other = lax.ppermute(mine, "row", cores)
    tokens_out, back = call(
        attend_kernel,
        (shape_of((tokens, CS), BF16), shape_of((tokens, CA), BF16)),
        mine,
        other,
        query,
        biased,
        gate,
        state,
        token_out,
        back_weight,
        hbm=(token_proj,),
        limit=50,
        scratch=(pltpu.VMEM((CS, CS), BF16), pltpu.SemaphoreType.DMA),
    )
    back_far = lax.ppermute(back, "row", far)
    back_core = lax.ppermute(back, "row", cores)
    atoms_out = call(
        spread_kernel,
        shape_of((rows, CA), BF16),
        mid,
        back,
        back_core,
        back_far,
        pick,
    )
    return (atoms_out, tokens_out)


def solution(mesh):
    split = P(("groups", "row"), None)
    line = P(("groups", "row"))
    return jax.shard_map(
        shards,
        mesh=mesh,
        in_specs=(split, line, line, line, line, split, P(("groups", "row"), None, None))
        + (P(),) * 12,
        out_specs=(split, split),
        check_vma=False,
    )
```

```python
import functools
import math

import jax
import jax.numpy as jnp
from jax import lax
from jax.experimental import pallas as pl
from jax.experimental.pallas import tpu as pltpu
from jax.sharding import PartitionSpec as P

CA = 128
CS = 768
HEADS = 16
AHEADS = 4
RESTYPES = 32
QBLK = 32
KWIN = 128
HDIM = 48
ADIM = 32
HALF = 128
REACH = 64
VMEM_LIMIT = 24 * 1024 * 1024
COST = 2_000_000_000
EPS = 1e-05
NEG = -1e30
F32 = jnp.float32
BF16 = jnp.bfloat16
COUNT, CHAIN, RES, WIN = 0, 16, 32, 48
TABLE = 128


def dot(a, b):
    return lax.dot_general(a, b, (((1,), (0,)), ((), ())), preferred_element_type=F32)


def dot_nt(a, b):
    return lax.dot_general(a, b, (((1,), (1,)), ((), ())), preferred_element_type=F32)


def norm(x, gain):
    centered = x - jnp.mean(x, axis=-1, keepdims=True)
    variance = jnp.mean(centered * centered, axis=-1, keepdims=True)
    return centered * lax.rsqrt(variance + EPS) * gain


def iota(shape, axis):
    return lax.broadcasted_iota(jnp.int32, shape, axis)


def table_row(table, row):
    return jnp.sum(jnp.where(iota(table.shape, 0) == row, table, 0), axis=0, keepdims=True)


def column(row, base, size):
    shape = (size, row.shape[1])
    return jnp.sum(jnp.where(iota(shape, 1) == iota(shape, 0) + base, row, 0), axis=1, keepdims=True)


def atoms_before(table, row, tokens):
    keep = (iota(table.shape, 0) < row) & (iota(table.shape, 1) < COUNT + tokens)
    return jnp.sum(jnp.sum(jnp.where(keep, table, 0), axis=0, keepdims=True), axis=1, keepdims=True)


def table_kernel(row_ref, table_ref):
    table_ref[...] = jnp.broadcast_to(row_ref[...][None], table_ref.shape)


def pair_kernel(pair_ref, gain_ref, weight_ref, bias_ref):
    gain, weight = gain_ref[...], weight_ref[...]
    for t in range(pair_ref.shape[0]):
        normed = norm(pair_ref[t].astype(F32), gain).astype(BF16)
        bias_ref[t * HEADS : (t + 1) * HEADS, :] = dot_nt(weight, normed)


def attend_window(queries, keys, values, start, begin, atoms):
    count, extent = queries.shape[0], keys.shape[0]
    head = iota((count, CA), 1) // ADIM
    stacked = jnp.concatenate(
        [jnp.where(head == h, queries, jnp.zeros_like(queries)) for h in range(AHEADS)], axis=0
    )
    scores = dot_nt(stacked, keys) * (1.0 / math.sqrt(ADIM))
    place = iota((count, extent), 1) + begin
    inside = (place >= start) & (place < start + KWIN) & (place >= 0) & (place < atoms)
    inside = jnp.concatenate([inside.astype(F32)] * AHEADS, axis=0) > 0.5
    scores = jnp.where(inside, scores, NEG)
    weights = jnp.exp(scores - jnp.max(scores, axis=-1, keepdims=True))
    denom = jnp.sum(weights, axis=-1, keepdims=True)
    mixed = dot(weights.astype(BF16), values) / denom
    total = jnp.zeros((count, CA), F32)
    for h in range(AHEADS):
        total = total + jnp.where(head == h, mixed[h * count : (h + 1) * count], 0.0)
    return total.astype(BF16)


def block_starts(row, count, first):
    shape = (count, row.shape[1])
    lane = iota(shape, 1) - first
    return jnp.sum(jnp.where(lane == iota(shape, 0) // QBLK, row, 0), axis=1, keepdims=True)


def edges(feat_core, feat_far, rows):
    even = lax.rem(lax.axis_index("row"), 2) == 0
    left = jnp.where(even, feat_far[rows - HALF :, :], feat_core[rows - HALF :, :])
    right = jnp.where(even, feat_core[:HALF, :], feat_far[:HALF, :])
    return left, right


def atom_kernel(
    n, feat_ref, core_ref, far_ref, window_ref, gain_ref, qkv_ref, out_ref, pool_ref, bias_ref,
    proj_ref, mid_ref, lifted_ref,
):
    me = lax.axis_index("row")
    rows = feat_ref.shape[0]
    left, right = edges(core_ref[...], far_ref[...], rows)
    feat = jnp.concatenate([left, feat_ref[...], right], axis=0).astype(F32)
    proj = dot(norm(feat, gain_ref[...]).astype(BF16), qkv_ref[...]).astype(BF16)
    proj_ref[...] = proj
    for s in range(rows // HALF):
        own = slice(HALF * s, HALF * s + HALF)
        ext = slice(HALF * s + HALF, HALF * s + 2 * HALF)
        near = slice(HALF * s + HALF - REACH, HALF * s + 3 * HALF - REACH)
        mixed = attend_window(
            proj[ext, :CA],
            proj[near, CA : 2 * CA],
            proj[near, 2 * CA :],
            block_starts(window_ref[...], HALF, s * HALF // QBLK),
            me * rows + HALF * s - REACH,
            n * rows,
        )
        mid = (feat[ext] + dot(mixed, out_ref[...])).astype(BF16)
        mid_ref[own, :] = mid
        lifted_ref[own, :] = jnp.maximum(dot(mid, pool_ref[...]), 0.0).astype(BF16)


def state_kernel(
    n, proj_ref, lifted_ref, core_ref, far_ref, table_ref, single_ref, out_ref, pool_ref, restype_ref, gain_ref,
    state_ref, normed_ref,
):
    me = lax.axis_index("row")
    rows = lifted_ref.shape[0]
    tokens = single_ref.shape[0]
    table = table_ref[...]
    own_row = table_row(table, me)
    windows = rows // QBLK
    size = 2 * HALF
    mixed = []
    for at, base, row, first in (
        (HALF - REACH, 0, me - 1, windows - REACH // QBLK),
        (HALF + rows, rows + 2 * HALF - size, me + 1, 0),
    ):
        mixed.append(
            attend_window(
                proj_ref[at : at + REACH, :CA],
                proj_ref[base : base + size, CA : 2 * CA],
                proj_ref[base : base + size, 2 * CA :],
                block_starts(table_row(table, row), REACH, WIN + first),
                me * rows - HALF + base,
                n * rows,
            )
        )
    left, right = edges(core_ref[...], far_ref[...], rows)
    feat = jnp.concatenate([left[HALF - REACH :], right[:REACH]], axis=0).astype(F32)
    mid = (feat + dot(jnp.concatenate(mixed, axis=0), out_ref[...])).astype(BF16)
    beside = jnp.maximum(dot(mid, pool_ref[...]), 0.0).astype(BF16)
    count = column(own_row, COUNT, tokens)
    shape = (tokens, TABLE)
    ahead = (iota(shape, 1) >= COUNT) & (iota(shape, 1) < COUNT + iota(shape, 0))
    begin = atoms_before(table, me, tokens) - me * rows
    begin = begin + jnp.sum(jnp.where(ahead, own_row, 0), axis=1, keepdims=True)
    atom = iota((tokens, rows), 1)
    chosen = (atom >= begin) & (atom < begin + count)
    pooled = dot(jnp.where(chosen, 1.0, 0.0).astype(BF16), lifted_ref[...])
    lane = iota((tokens, 2 * REACH), 1)
    atom = jnp.where(lane < REACH, lane - REACH, lane - REACH + rows)
    chosen = (atom >= begin) & (atom < begin + count)
    pooled = pooled + dot(jnp.where(chosen, 1.0, 0.0).astype(BF16), beside)
    kind = column(own_row, RES, tokens)
    onehot = jnp.where(iota((tokens, RESTYPES), 1) == kind, 1.0, 0.0).astype(BF16)
    state = single_ref[...].astype(F32) + pooled / count.astype(F32)
    state = state + dot(onehot, restype_ref[...])
    state_ref[...] = state
    token_normed = norm(state, gain_ref[...]).astype(BF16)
    for i in range(normed_ref.shape[0]):
        normed_ref[i] = token_normed


def query_kernel(
    normed_ref, table_ref, bias_ref, chain_weight_ref, proj_ref,
    query_ref, gate_ref, biased_ref, pick_ref, wv_ref,
    sem,
):
    copy = pltpu.make_async_copy(proj_ref.at[:, pl.ds(2 * CS, CS)], wv_ref, sem)
    copy.start()
    me = lax.axis_index("row")
    normed = normed_ref[0]
    tokens = normed.shape[0]
    query = dot(normed, proj_ref[:, :CS]).astype(BF16)
    head = iota((HEADS, CS), 1) // HDIM == iota((HEADS, CS), 0)
    spread = jnp.concatenate(
        [
            jnp.where(head, jnp.broadcast_to(query[t : t + 1].astype(F32), (HEADS, CS)), 0.0)
            for t in range(tokens)
        ],
        axis=0,
    ).astype(BF16)
    query_ref[...] = dot_nt(spread, proj_ref[:, CS : 2 * CS]).astype(BF16)
    table = table_ref[...]
    n = table.shape[0]
    keys = n * tokens
    shape = (TABLE, keys)
    pick = jnp.where(iota(shape, 0) == CHAIN + iota(shape, 1) % tokens, 1.0, 0.0).astype(BF16)
    each = dot(table.astype(F32).astype(BF16), pick)
    shape = (n, keys)
    chain_keys = jnp.sum(
        jnp.where(iota(shape, 1) // tokens == iota(shape, 0), each, 0.0), axis=0, keepdims=True
    )
    own_row = table_row(table, me)
    shape = (tokens * HEADS, TABLE)
    mine = iota(shape, 1) == CHAIN + iota(shape, 0) // HEADS
    chain_rows = jnp.sum(jnp.where(mine, own_row, 0), axis=1, keepdims=True).astype(F32)
    shape = (tokens * HEADS, HEADS)
    mine = iota(shape, 1) == iota(shape, 0) % HEADS
    weight = jnp.sum(jnp.where(mine, chain_weight_ref[...], 0.0), axis=1, keepdims=True)
    biased_ref[...] = bias_ref[...] + jnp.where(chain_rows == chain_keys, weight, 0.0)
    rows = pick_ref.shape[0]
    counts = jnp.where(iota(table.shape, 1) < COUNT + tokens, table, 0).astype(F32).astype(BF16)
    begin = jnp.zeros((1, TABLE), F32)
    size = jnp.zeros((1, TABLE), F32)
    for step in range(3):
        shape = (TABLE, TABLE)
        token = iota(shape, 1) - step * tokens
        here = (token >= 0) & (token < tokens)
        ahead = jnp.where(here & (iota(shape, 0) < COUNT + token), 1.0, 0.0).astype(BF16)
        equal = jnp.where(here & (iota(shape, 0) == COUNT + token), 1.0, 0.0).astype(BF16)
        at = iota(table.shape, 0) == me + step - 1
        begin += jnp.sum(jnp.where(at, dot(counts, ahead), 0.0), axis=0, keepdims=True)
        size += jnp.sum(jnp.where(at, dot(counts, equal), 0.0), axis=0, keepdims=True)
        before = atoms_before(table, me + step - 1, tokens).astype(F32)
        begin += jnp.where(here[:1], before, 0.0)
    atom = (iota((rows, TABLE), 0) + me * rows).astype(F32)
    pick_ref[...] = jnp.where((atom >= begin) & (atom < begin + size), 1.0, 0.0).astype(BF16)
    gate_ref[...] = jax.nn.sigmoid(dot(normed, proj_ref[:, 3 * CS :]))
    copy.wait()


def attend_kernel(
    mine_ref, other_ref, query_ref, biased_ref, gate_ref, state_ref, wv_ref, out_ref, tokens_ref, copy_ref
):
    even = lax.rem(lax.axis_index("row"), 2) == 0
    tokens = state_ref.shape[0]
    chips = mine_ref.shape[0]
    mine, other = mine_ref[...], other_ref[...]
    first = jnp.where(even, mine, other)
    second = jnp.where(even, other, mine)
    normed = jnp.concatenate(
        [part[c] for c in range(chips) for part in (first, second)], axis=0
    )
    scores = dot_nt(query_ref[...], normed) * (1.0 / math.sqrt(HDIM)) + biased_ref[...]
    weights = jnp.exp(scores - jnp.max(scores, axis=-1, keepdims=True))
    denom = jnp.sum(weights, axis=-1, keepdims=True)
    values = dot(normed, wv_ref[...]).astype(BF16)
    mixed = dot(weights.astype(BF16), values) / denom
    head = iota((HEADS, CS), 1) // HDIM == iota((HEADS, CS), 0)
    mixed = jnp.concatenate(
        [
            jnp.sum(
                jnp.where(head, mixed[t * HEADS : (t + 1) * HEADS], 0.0), axis=0, keepdims=True
            )
            for t in range(tokens)
        ],
        axis=0,
    )
    gated = (mixed * gate_ref[...]).astype(BF16)
    updated = (state_ref[...] + dot(gated, out_ref[...])).astype(BF16)
    tokens_ref[...] = updated
    copy_ref[...] = updated


def spread_kernel(mid_ref, own_ref, core_ref, far_ref, pick_ref, weight_ref, atoms_ref):
    even = lax.rem(lax.axis_index("row"), 2) == 0
    core, far, own = core_ref[...], far_ref[...], own_ref[...]
    parts = [jnp.where(even, far, core), own, jnp.where(even, core, far)]
    back = dot(jnp.concatenate(parts, axis=0), weight_ref[...]).astype(BF16)
    rest = jnp.zeros((TABLE - back.shape[0], CA), BF16)
    spread = dot(pick_ref[...], jnp.concatenate([back, rest], axis=0))
    atoms_ref[...] = (mid_ref[...].astype(F32) + spread).astype(BF16)


def call(kernel, outs, *args, scratch=(), aliases=None):
    spec = pl.BlockSpec(memory_space=pltpu.VMEM)
    return pl.pallas_call(
        kernel,
        out_shape=outs,
        in_specs=[spec] * len(args),
        out_specs=jax.tree.map(lambda _: spec, outs),
        scratch_shapes=list(scratch),
        input_output_aliases=aliases or {},
        compiler_params=pltpu.CompilerParams(vmem_limit_bytes=VMEM_LIMIT),
        cost_estimate=pl.CostEstimate(flops=COST, bytes_accessed=COST // 200, transcendentals=0),
    )(*args)


def shape_of(shape, dtype):
    return jax.ShapeDtypeStruct(shape, dtype)


def shards(
    atom_feat,
    window_start,
    atom_count,
    residue_type,
    chain_id,
    token_single,
    pair,
    atom_gain,
    atom_qkv,
    atom_out,
    pool_weight,
    restype_table,
    token_gain,
    token_proj,
    token_out,
    pair_gain,
    pair_bias_weight,
    chain_weight,
    back_weight,
):
    n = lax.axis_size("row")
    rows, tokens, extent = atom_feat.shape[0], token_single.shape[0], pair.shape[1]
    cores = [(i, i ^ 1) for i in range(n)]
    far = [(i, i + 1) for i in range(1, n - 1, 2)] + [(i + 1, i) for i in range(1, n - 1, 2)]
    same_core = [[2 * c + core for c in range(n // 2)] for core in range(2)]

    feat_far = lax.ppermute(atom_feat, "row", far)
    feat_core = lax.ppermute(atom_feat, "row", cores)
    ints = jnp.concatenate([atom_count, chain_id, residue_type, window_start])
    ints = jnp.pad(ints, (0, TABLE - ints.shape[0]))[None]
    table = call(table_kernel, shape_of((n, 1, TABLE), jnp.int32), ints)
    table = lax.all_to_all(table, "row", 0, 0, tiled=True).reshape(n, TABLE)

    bias = call(
        pair_kernel, shape_of((tokens * HEADS, extent), F32), pair, pair_gain, pair_bias_weight.T
    )
    proj, mid, lifted = call(
        functools.partial(atom_kernel, n),
        (
            shape_of((rows + 2 * HALF, 3 * CA), BF16),
            shape_of((rows, CA), BF16),
            shape_of((rows, CS), BF16),
        ),
        atom_feat,
        feat_core,
        feat_far,
        window_start[None],
        atom_gain,
        atom_qkv,
        atom_out,
        pool_weight,
        bias,
    )
    state, normed = call(
        functools.partial(state_kernel, n),
        (shape_of((tokens, CS), F32), shape_of((n // 2, tokens, CS), BF16)),
        proj,
        lifted,
        feat_core,
        feat_far,
        table,
        token_single,
        atom_out,
        pool_weight,
        restype_table,
        token_gain,
    )
    mine = lax.all_to_all(normed, "row", 0, 0, tiled=True, axis_index_groups=same_core)
    query, gate, biased, pick, wv = call(
        query_kernel,
        (
            shape_of((tokens * HEADS, CS), BF16),
            shape_of((tokens, CS), F32),
            shape_of((tokens * HEADS, extent), F32),
            shape_of((rows, TABLE), BF16),
            shape_of((CS, CS), BF16),
        ),
        normed,
        table,
        bias,
        chain_weight,
        token_proj,
        scratch=(pltpu.SemaphoreType.DMA,),
        aliases={2: 2},
    )
    mine, query = lax.optimization_barrier((mine, query))
    other = lax.ppermute(mine, "row", cores)
    tokens_out, updated = call(
        attend_kernel,
        (shape_of((tokens, CS), BF16), shape_of((tokens, CS), BF16)),
        mine,
        other,
        query,
        biased,
        gate,
        state,
        wv,
        token_out,
    )
    tokens_far = lax.ppermute(updated, "row", far)
    tokens_core = lax.ppermute(updated, "row", cores)
    atoms_out = call(
        spread_kernel,
        shape_of((rows, CA), BF16),
        mid,
        updated,
        tokens_core,
        tokens_far,
        pick,
        back_weight,
    )
    return (atoms_out, tokens_out)


def solution(mesh):
    split = P(("groups", "row"), None)
    line = P(("groups", "row"))
    return jax.shard_map(
        shards,
        mesh=mesh,
        in_specs=(split, line, line, line, line, split, P(("groups", "row"), None, None))
        + (P(),) * 12,
        out_specs=(split, split),
        check_vma=False,
    )
```

```python
import functools
import math

import jax
import jax.numpy as jnp
from jax import lax
from jax.experimental import pallas as pl
from jax.experimental.pallas import tpu as pltpu
from jax.sharding import PartitionSpec as P

CA = 128
CS = 768
HEADS = 16
AHEADS = 4
RESTYPES = 32
QBLK = 32
KWIN = 128
HDIM = 48
ADIM = 32
HALF = 128
REACH = 64
VMEM_LIMIT = 24 * 1024 * 1024
COST = 2_000_000_000
EPS = 1e-05
NEG = -1e30
F32 = jnp.float32
BF16 = jnp.bfloat16
COUNT, CHAIN, RES, WIN = 0, 16, 32, 48
TABLE = 128


def dot(a, b):
    return lax.dot_general(a, b, (((1,), (0,)), ((), ())), preferred_element_type=F32)


def dot_nt(a, b):
    return lax.dot_general(a, b, (((1,), (1,)), ((), ())), preferred_element_type=F32)


def norm(x, gain):
    centered = x - jnp.mean(x, axis=-1, keepdims=True)
    variance = jnp.mean(centered * centered, axis=-1, keepdims=True)
    return centered * lax.rsqrt(variance + EPS) * gain


def iota(shape, axis):
    return lax.broadcasted_iota(jnp.int32, shape, axis)


def table_row(table, row):
    return jnp.sum(jnp.where(iota(table.shape, 0) == row, table, 0), axis=0, keepdims=True)


def column(row, base, size):
    shape = (size, row.shape[1])
    return jnp.sum(jnp.where(iota(shape, 1) == iota(shape, 0) + base, row, 0), axis=1, keepdims=True)


def atoms_before(table, row, tokens):
    keep = (iota(table.shape, 0) < row) & (iota(table.shape, 1) < COUNT + tokens)
    return jnp.sum(jnp.sum(jnp.where(keep, table, 0), axis=0, keepdims=True), axis=1, keepdims=True)


def first_kernel(out_ref):
    out_ref[...] = jnp.zeros_like(out_ref)


def table_kernel(zero_ref, count_ref, chain_ref, kind_ref, window_ref, table_ref):
    row = zero_ref[:1]
    pieces = ((COUNT, count_ref), (CHAIN, chain_ref), (RES, kind_ref), (WIN, window_ref))
    for base, ref in pieces:
        size = ref.shape[1]
        shape = (size, TABLE)
        at = iota(shape, 1) == iota(shape, 0) + base
        eye = iota((size, size), 0) == iota((size, size), 1)
        values = jnp.sum(jnp.where(eye, ref[...], 0), axis=1, keepdims=True)
        row = row + jnp.sum(jnp.where(at, values, 0), axis=0, keepdims=True)
    table_ref[...] = jnp.broadcast_to(row[None], table_ref.shape)


def pair_kernel(pair_ref, gain_ref, weight_ref, bias_ref):
    gain, weight = gain_ref[...], weight_ref[...]
    for t in range(pair_ref.shape[0]):
        normed = norm(pair_ref[t].astype(F32), gain).astype(BF16)
        bias_ref[t * HEADS : (t + 1) * HEADS, :] = dot_nt(weight, normed)


def attend_window(queries, keys, values, start, begin, atoms):
    count, extent = queries.shape[0], keys.shape[0]
    head = iota((count, CA), 1) // ADIM
    stacked = jnp.concatenate(
        [jnp.where(head == h, queries, jnp.zeros_like(queries)) for h in range(AHEADS)], axis=0
    )
    scores = dot_nt(stacked, keys) * (1.0 / math.sqrt(ADIM))
    place = iota((count, extent), 1) + begin
    inside = (place >= start) & (place < start + KWIN) & (place >= 0) & (place < atoms)
    inside = jnp.concatenate([inside.astype(F32)] * AHEADS, axis=0) > 0.5
    scores = jnp.where(inside, scores, NEG)
    weights = jnp.exp(scores - jnp.max(scores, axis=-1, keepdims=True))
    denom = jnp.sum(weights, axis=-1, keepdims=True)
    mixed = dot(weights.astype(BF16), values) / denom
    total = jnp.zeros((count, CA), F32)
    for h in range(AHEADS):
        total = total + jnp.where(head == h, mixed[h * count : (h + 1) * count], 0.0)
    return total.astype(BF16)


def block_starts(row, count, first):
    shape = (count, row.shape[1])
    lane = iota(shape, 1) - first
    return jnp.sum(jnp.where(lane == iota(shape, 0) // QBLK, row, 0), axis=1, keepdims=True)


def edges(feat_core, feat_far, rows):
    even = lax.rem(lax.axis_index("row"), 2) == 0
    left = jnp.where(even, feat_far[rows - HALF :, :], feat_core[rows - HALF :, :])
    right = jnp.where(even, feat_core[:HALF, :], feat_far[:HALF, :])
    return left, right


def atom_kernel(
    n, feat_ref, core_ref, far_ref, window_ref, gain_ref, qkv_ref, out_ref, pool_ref, bias_ref,
    proj_ref, mid_ref, lifted_ref,
):
    me = lax.axis_index("row")
    rows = feat_ref.shape[0]
    left, right = edges(core_ref[...], far_ref[...], rows)
    feat = jnp.concatenate([left, feat_ref[...], right], axis=0).astype(F32)
    proj = dot(norm(feat, gain_ref[...]).astype(BF16), qkv_ref[...]).astype(BF16)
    proj_ref[...] = proj
    for s in range(rows // HALF):
        own = slice(HALF * s, HALF * s + HALF)
        ext = slice(HALF * s + HALF, HALF * s + 2 * HALF)
        near = slice(HALF * s + HALF - REACH, HALF * s + 3 * HALF - REACH)
        mixed = attend_window(
            proj[ext, :CA],
            proj[near, CA : 2 * CA],
            proj[near, 2 * CA :],
            block_starts(window_ref[...], HALF, s * HALF // QBLK),
            me * rows + HALF * s - REACH,
            n * rows,
        )
        mid = (feat[ext] + dot(mixed, out_ref[...])).astype(BF16)
        mid_ref[own, :] = mid
        lifted_ref[own, :] = jnp.maximum(dot(mid, pool_ref[...]), 0.0).astype(BF16)


def state_kernel(
    n, proj_ref, lifted_ref, core_ref, far_ref, table_ref, single_ref, out_ref, pool_ref, restype_ref, gain_ref,
    state_ref, normed_ref,
):
    me = lax.axis_index("row")
    rows = lifted_ref.shape[0]
    tokens = single_ref.shape[0]
    table = table_ref[...]
    own_row = table_row(table, me)
    windows = rows // QBLK
    size = 2 * HALF
    mixed = []
    for at, base, row, first in (
        (HALF - REACH, 0, me - 1, windows - REACH // QBLK),
        (HALF + rows, rows + 2 * HALF - size, me + 1, 0),
    ):
        mixed.append(
            attend_window(
                proj_ref[at : at + REACH, :CA],
                proj_ref[base : base + size, CA : 2 * CA],
                proj_ref[base : base + size, 2 * CA :],
                block_starts(table_row(table, row), REACH, WIN + first),
                me * rows - HALF + base,
                n * rows,
            )
        )
    left, right = edges(core_ref[...], far_ref[...], rows)
    feat = jnp.concatenate([left[HALF - REACH :], right[:REACH]], axis=0).astype(F32)
    mid = (feat + dot(jnp.concatenate(mixed, axis=0), out_ref[...])).astype(BF16)
    beside = jnp.maximum(dot(mid, pool_ref[...]), 0.0).astype(BF16)
    count = column(own_row, COUNT, tokens)
    shape = (tokens, TABLE)
    ahead = (iota(shape, 1) >= COUNT) & (iota(shape, 1) < COUNT + iota(shape, 0))
    begin = atoms_before(table, me, tokens) - me * rows
    begin = begin + jnp.sum(jnp.where(ahead, own_row, 0), axis=1, keepdims=True)
    atom = iota((tokens, rows), 1)
    chosen = (atom >= begin) & (atom < begin + count)
    pooled = dot(jnp.where(chosen, 1.0, 0.0).astype(BF16), lifted_ref[...])
    lane = iota((tokens, 2 * REACH), 1)
    atom = jnp.where(lane < REACH, lane - REACH, lane - REACH + rows)
    chosen = (atom >= begin) & (atom < begin + count)
    pooled = pooled + dot(jnp.where(chosen, 1.0, 0.0).astype(BF16), beside)
    kind = column(own_row, RES, tokens)
    onehot = jnp.where(iota((tokens, RESTYPES), 1) == kind, 1.0, 0.0).astype(BF16)
    state = single_ref[...].astype(F32) + pooled / count.astype(F32)
    state = state + dot(onehot, restype_ref[...])
    state_ref[...] = state
    token_normed = norm(state, gain_ref[...]).astype(BF16)
    for i in range(normed_ref.shape[0]):
        normed_ref[i] = token_normed


def query_kernel(
    normed_ref, table_ref, bias_ref, chain_weight_ref, proj_ref,
    query_ref, gate_ref, biased_ref, pick_ref, wv_ref,
    sem,
):
    copy = pltpu.make_async_copy(proj_ref.at[:, pl.ds(2 * CS, CS)], wv_ref, sem)
    copy.start()
    me = lax.axis_index("row")
    normed = normed_ref[0]
    tokens = normed.shape[0]
    query = dot(normed, proj_ref[:, :CS]).astype(BF16)
    head = iota((HEADS, CS), 1) // HDIM == iota((HEADS, CS), 0)
    spread = jnp.concatenate(
        [
            jnp.where(head, jnp.broadcast_to(query[t : t + 1].astype(F32), (HEADS, CS)), 0.0)
            for t in range(tokens)
        ],
        axis=0,
    ).astype(BF16)
    query_ref[...] = dot_nt(spread, proj_ref[:, CS : 2 * CS]).astype(BF16)
    table = table_ref[...]
    n = table.shape[0]
    keys = n * tokens
    shape = (TABLE, keys)
    pick = jnp.where(iota(shape, 0) == CHAIN + iota(shape, 1) % tokens, 1.0, 0.0).astype(BF16)
    each = dot(table.astype(F32).astype(BF16), pick)
    shape = (n, keys)
    chain_keys = jnp.sum(
        jnp.where(iota(shape, 1) // tokens == iota(shape, 0), each, 0.0), axis=0, keepdims=True
    )
    own_row = table_row(table, me)
    shape = (tokens * HEADS, TABLE)
    mine = iota(shape, 1) == CHAIN + iota(shape, 0) // HEADS
    chain_rows = jnp.sum(jnp.where(mine, own_row, 0), axis=1, keepdims=True).astype(F32)
    shape = (tokens * HEADS, HEADS)
    mine = iota(shape, 1) == iota(shape, 0) % HEADS
    weight = jnp.sum(jnp.where(mine, chain_weight_ref[...], 0.0), axis=1, keepdims=True)
    biased_ref[...] = bias_ref[...] + jnp.where(chain_rows == chain_keys, weight, 0.0)
    rows = pick_ref.shape[0]
    counts = jnp.where(iota(table.shape, 1) < COUNT + tokens, table, 0).astype(F32).astype(BF16)
    begin = jnp.zeros((1, TABLE), F32)
    size = jnp.zeros((1, TABLE), F32)
    for step in range(3):
        shape = (TABLE, TABLE)
        token = iota(shape, 1) - step * tokens
        here = (token >= 0) & (token < tokens)
        ahead = jnp.where(here & (iota(shape, 0) < COUNT + token), 1.0, 0.0).astype(BF16)
        equal = jnp.where(here & (iota(shape, 0) == COUNT + token), 1.0, 0.0).astype(BF16)
        at = iota(table.shape, 0) == me + step - 1
        begin += jnp.sum(jnp.where(at, dot(counts, ahead), 0.0), axis=0, keepdims=True)
        size += jnp.sum(jnp.where(at, dot(counts, equal), 0.0), axis=0, keepdims=True)
        before = atoms_before(table, me + step - 1, tokens).astype(F32)
        begin += jnp.where(here[:1], before, 0.0)
    atom = (iota((rows, TABLE), 0) + me * rows).astype(F32)
    pick_ref[...] = jnp.where((atom >= begin) & (atom < begin + size), 1.0, 0.0).astype(BF16)
    gate_ref[...] = jax.nn.sigmoid(dot(normed, proj_ref[:, 3 * CS :]))
    copy.wait()


def attend_kernel(
    mine_ref, other_ref, query_ref, biased_ref, gate_ref, state_ref, wv_ref, out_ref, tokens_ref
):
    even = lax.rem(lax.axis_index("row"), 2) == 0
    tokens = state_ref.shape[0]
    chips = mine_ref.shape[0]
    mine, other = mine_ref[...], other_ref[...]
    first = jnp.where(even, mine, other)
    second = jnp.where(even, other, mine)
    normed = jnp.concatenate(
        [part[c] for c in range(chips) for part in (first, second)], axis=0
    )
    scores = dot_nt(query_ref[...], normed) * (1.0 / math.sqrt(HDIM)) + biased_ref[...]
    weights = jnp.exp(scores - jnp.max(scores, axis=-1, keepdims=True))
    denom = jnp.sum(weights, axis=-1, keepdims=True)
    values = dot(normed, wv_ref[...]).astype(BF16)
    mixed = dot(weights.astype(BF16), values) / denom
    head = iota((HEADS, CS), 1) // HDIM == iota((HEADS, CS), 0)
    mixed = jnp.concatenate(
        [
            jnp.sum(
                jnp.where(head, mixed[t * HEADS : (t + 1) * HEADS], 0.0), axis=0, keepdims=True
            )
            for t in range(tokens)
        ],
        axis=0,
    )
    gated = (mixed * gate_ref[...]).astype(BF16)
    tokens_ref[...] = (state_ref[...] + dot(gated, out_ref[...])).astype(BF16)


def own_kernel(mid_ref, own_ref, pick_ref, weight_ref, back_ref, partial_ref, tokens_ref):
    own = own_ref[...]
    tokens_ref[...] = own
    back = dot(own, weight_ref[...]).astype(BF16)
    back_ref[...] = back
    count = back.shape[0]
    rest = jnp.zeros((TABLE - 2 * count, CA), BF16)
    spread = dot(pick_ref[...], jnp.concatenate([jnp.zeros_like(back), back, rest], axis=0))
    partial_ref[...] = mid_ref[...].astype(F32) + spread


def beside_kernel(partial_ref, core_ref, far_ref, pick_ref, weight_ref, atoms_ref):
    even = lax.rem(lax.axis_index("row"), 2) == 0
    core, far = core_ref[...], dot(far_ref[...], weight_ref[...]).astype(BF16)
    parts = [jnp.where(even, far, core), jnp.zeros_like(core), jnp.where(even, core, far)]
    rest = jnp.zeros((TABLE - 3 * core.shape[0], CA), BF16)
    spread = dot(pick_ref[...], jnp.concatenate([*parts, rest], axis=0))
    atoms_ref[...] = (partial_ref[...] + spread).astype(BF16)


def call(kernel, outs, *args, scratch=(), aliases=None):
    spec = pl.BlockSpec(memory_space=pltpu.VMEM)
    return pl.pallas_call(
        kernel,
        out_shape=outs,
        in_specs=[spec] * len(args),
        out_specs=jax.tree.map(lambda _: spec, outs),
        scratch_shapes=list(scratch),
        input_output_aliases=aliases or {},
        compiler_params=pltpu.CompilerParams(vmem_limit_bytes=VMEM_LIMIT),
        cost_estimate=pl.CostEstimate(flops=COST, bytes_accessed=COST // 200, transcendentals=0),
    )(*args)


def shape_of(shape, dtype):
    return jax.ShapeDtypeStruct(shape, dtype)


def shards(
    atom_feat,
    window_start,
    atom_count,
    residue_type,
    chain_id,
    token_single,
    pair,
    atom_gain,
    atom_qkv,
    atom_out,
    pool_weight,
    restype_table,
    token_gain,
    token_proj,
    token_out,
    pair_gain,
    pair_bias_weight,
    chain_weight,
    back_weight,
):
    n = lax.axis_size("row")
    rows, tokens, extent = atom_feat.shape[0], token_single.shape[0], pair.shape[1]
    cores = [(i, i ^ 1) for i in range(n)]
    far = [(i, i + 1) for i in range(1, n - 1, 2)] + [(i + 1, i) for i in range(1, n - 1, 2)]
    same_core = [[2 * c + core for c in range(n // 2)] for core in range(2)]

    feat_far = lax.ppermute(atom_feat, "row", far)
    feat_core = lax.ppermute(atom_feat, "row", cores)
    table = call(
        table_kernel,
        shape_of((n, 1, TABLE), jnp.int32),
        call(first_kernel, shape_of((8, TABLE), jnp.int32)),
        atom_count[None],
        chain_id[None],
        residue_type[None],
        window_start[None],
    )
    table = lax.all_to_all(table, "row", 0, 0, tiled=True).reshape(n, TABLE)

    bias = call(
        pair_kernel, shape_of((tokens * HEADS, extent), F32), pair, pair_gain, pair_bias_weight.T
    )
    proj, mid, lifted = call(
        functools.partial(atom_kernel, n),
        (
            shape_of((rows + 2 * HALF, 3 * CA), BF16),
            shape_of((rows, CA), BF16),
            shape_of((rows, CS), BF16),
        ),
        atom_feat,
        feat_core,
        feat_far,
        window_start[None],
        atom_gain,
        atom_qkv,
        atom_out,
        pool_weight,
        bias,
    )
    state, normed = call(
        functools.partial(state_kernel, n),
        (shape_of((tokens, CS), F32), shape_of((n // 2, tokens, CS), BF16)),
        proj,
        lifted,
        feat_core,
        feat_far,
        table,
        token_single,
        atom_out,
        pool_weight,
        restype_table,
        token_gain,
    )
    mine = lax.all_to_all(normed, "row", 0, 0, tiled=True, axis_index_groups=same_core)
    query, gate, biased, pick, wv = call(
        query_kernel,
        (
            shape_of((tokens * HEADS, CS), BF16),
            shape_of((tokens, CS), F32),
            shape_of((tokens * HEADS, extent), F32),
            shape_of((rows, TABLE), BF16),
            shape_of((CS, CS), BF16),
        ),
        normed,
        table,
        bias,
        chain_weight,
        token_proj,
        scratch=(pltpu.SemaphoreType.DMA,),
        aliases={2: 2},
    )
    mine, query = lax.optimization_barrier((mine, query))
    other = lax.ppermute(mine, "row", cores)
    updated = call(
        attend_kernel,
        shape_of((tokens, CS), BF16),
        mine,
        other,
        query,
        biased,
        gate,
        state,
        wv,
        token_out,
    )
    tokens_far = lax.ppermute(updated, "row", far)
    back, partial, tokens_out = call(
        own_kernel,
        (shape_of((tokens, CA), BF16), shape_of((rows, CA), F32), shape_of((tokens, CS), BF16)),
        mid,
        updated,
        pick,
        back_weight,
    )
    back_core = lax.ppermute(back, "row", cores)
    atoms_out = call(
        beside_kernel,
        shape_of((rows, CA), BF16),
        partial,
        back_core,
        tokens_far,
        pick,
        back_weight,
    )
    return (atoms_out, tokens_out)


def solution(mesh):
    split = P(("groups", "row"), None)
    line = P(("groups", "row"))
    return jax.shard_map(
        shards,
        mesh=mesh,
        in_specs=(split, line, line, line, line, split, P(("groups", "row"), None, None))
        + (P(),) * 12,
        out_specs=(split, split),
        check_vma=False,
    )
```

```python
import functools
import math

import jax
import jax.numpy as jnp
from jax import lax
from jax.experimental import pallas as pl
from jax.experimental.pallas import tpu as pltpu
from jax.sharding import PartitionSpec as P

CA = 128
CS = 768
HEADS = 16
AHEADS = 4
RESTYPES = 32
QBLK = 32
KWIN = 128
HDIM = 48
ADIM = 32
HALF = 128
REACH = 64
VMEM_LIMIT = 24 * 1024 * 1024
COST = 2_000_000_000
EPS = 1e-05
NEG = -1e30
F32 = jnp.float32
BF16 = jnp.bfloat16
TABLE = 128


def dot(a, b):
    return lax.dot_general(a, b, (((1,), (0,)), ((), ())), preferred_element_type=F32)


def dot_nt(a, b):
    return lax.dot_general(a, b, (((1,), (1,)), ((), ())), preferred_element_type=F32)


def norm(x, gain):
    centered = x - jnp.mean(x, axis=-1, keepdims=True)
    variance = jnp.mean(centered * centered, axis=-1, keepdims=True)
    return centered * lax.rsqrt(variance + EPS) * gain


def iota(shape, axis):
    return lax.broadcasted_iota(jnp.int32, shape, axis)


def table_row(table, row):
    return jnp.sum(jnp.where(iota(table.shape, 0) == row, table, 0), axis=0, keepdims=True)


def column(row, base, size):
    shape = (size, row.shape[1])
    return jnp.sum(jnp.where(iota(shape, 1) == iota(shape, 0) + base, row, 0), axis=1, keepdims=True)


def atoms_before(table, row, tokens):
    keep = (iota(table.shape, 0) < row) & (iota(table.shape, 1) < tokens)
    return jnp.sum(jnp.sum(jnp.where(keep, table, 0), axis=0, keepdims=True), axis=1, keepdims=True)


def first_kernel(out_ref):
    out_ref[...] = jnp.zeros_like(out_ref)


def table_kernel(zero_ref, count_ref, chain_ref, kind_ref, window_ref, table_ref):
    row = zero_ref[:1]
    pieces = (count_ref, chain_ref, kind_ref, window_ref)
    base = 0
    for ref in pieces:
        size = ref.shape[1]
        shape = (size, TABLE)
        at = iota(shape, 1) == iota(shape, 0) + base
        eye = iota((size, size), 0) == iota((size, size), 1)
        values = jnp.sum(jnp.where(eye, ref[...], 0), axis=1, keepdims=True)
        row = row + jnp.sum(jnp.where(at, values, 0), axis=0, keepdims=True)
        base += size
    table_ref[...] = jnp.broadcast_to(row[None], table_ref.shape)


def pair_kernel(pair_ref, gain_ref, weight_ref, bias_ref):
    gain, weight = gain_ref[...], weight_ref[...]
    for t in range(pair_ref.shape[0]):
        normed = norm(pair_ref[t].astype(F32), gain).astype(BF16)
        bias_ref[t * HEADS : (t + 1) * HEADS, :] = dot_nt(weight, normed)


def window_scores(queries, keys):
    head = iota(queries.shape, 1) // ADIM
    stacked = jnp.concatenate(
        [jnp.where(head == h, queries, jnp.zeros_like(queries)) for h in range(AHEADS)], axis=0
    )
    return dot_nt(stacked, keys) * (1.0 / math.sqrt(ADIM))


def attend_window(scores, values, start, begin, atoms):
    count, extent = scores.shape[0] // AHEADS, scores.shape[1]
    head = iota((count, CA), 1) // ADIM
    place = iota((count, extent), 1) + begin
    inside = (place >= start) & (place < start + KWIN) & (place >= 0) & (place < atoms)
    inside = jnp.concatenate([inside.astype(F32)] * AHEADS, axis=0) > 0.5
    scores = jnp.where(inside, scores, NEG)
    weights = jnp.exp(scores - jnp.max(scores, axis=-1, keepdims=True))
    denom = jnp.sum(weights, axis=-1, keepdims=True)
    mixed = dot(weights.astype(BF16), values) / denom
    total = jnp.zeros((count, CA), F32)
    for h in range(AHEADS):
        total = total + jnp.where(head == h, mixed[h * count : (h + 1) * count], 0.0)
    return total.astype(BF16)


def block_starts(row, count, first):
    shape = (count, row.shape[1])
    lane = iota(shape, 1) - first
    return jnp.sum(jnp.where(lane == iota(shape, 0) // QBLK, row, 0), axis=1, keepdims=True)


def edges(feat_core, feat_far, rows):
    even = lax.rem(lax.axis_index("row"), 2) == 0
    left = jnp.where(even, feat_far[rows - HALF :, :], feat_core[rows - HALF :, :])
    right = jnp.where(even, feat_core[:HALF, :], feat_far[:HALF, :])
    return left, right


def atom_kernel(
    n, feat_ref, core_ref, far_ref, window_ref, gain_ref, qkv_ref, out_ref, pool_ref, bias_ref,
    values_ref, scores_ref, mid_ref, lifted_ref,
):
    me = lax.axis_index("row")
    rows = feat_ref.shape[0]
    left, right = edges(core_ref[...], far_ref[...], rows)
    feat = jnp.concatenate([left, feat_ref[...], right], axis=0).astype(F32)
    proj = dot(norm(feat, gain_ref[...]).astype(BF16), qkv_ref[...]).astype(BF16)
    values_ref[...] = proj[:, 2 * CA :]
    for i, (at, base) in enumerate(((HALF - REACH, 0), (HALF + rows, rows))):
        part = window_scores(
            proj[at : at + REACH, :CA], proj[base : base + 2 * HALF, CA : 2 * CA]
        )
        scores_ref[i] = part
    for s in range(rows // HALF):
        own = slice(HALF * s, HALF * s + HALF)
        ext = slice(HALF * s + HALF, HALF * s + 2 * HALF)
        near = slice(HALF * s + HALF - REACH, HALF * s + 3 * HALF - REACH)
        mixed = attend_window(
            window_scores(proj[ext, :CA], proj[near, CA : 2 * CA]),
            proj[near, 2 * CA :],
            block_starts(window_ref[...], HALF, s * HALF // QBLK),
            me * rows + HALF * s - REACH,
            n * rows,
        )
        mid = (feat[ext] + dot(mixed, out_ref[...])).astype(BF16)
        mid_ref[own, :] = mid
        lifted_ref[own, :] = jnp.maximum(dot(mid, pool_ref[...]), 0.0).astype(BF16)


def state_kernel(
    n, values_ref, scores_ref, lifted_ref, core_ref, far_ref, table_ref, single_ref, out_ref, pool_ref, restype_ref, gain_ref,
    state_ref, normed_ref,
):
    me = lax.axis_index("row")
    rows = lifted_ref.shape[0]
    tokens = single_ref.shape[0]
    table = table_ref[...]
    own_row = table_row(table, me)
    windows = rows // QBLK
    mixed = []
    for i, (base, row, first) in enumerate(
        ((0, me - 1, windows - REACH // QBLK), (rows, me + 1, 0))
    ):
        mixed.append(
            attend_window(
                scores_ref[i],
                values_ref[base : base + 2 * HALF, :],
                block_starts(table_row(table, row), REACH, 3 * tokens + first),
                me * rows - HALF + base,
                n * rows,
            )
        )
    left, right = edges(core_ref[...], far_ref[...], rows)
    feat = jnp.concatenate([left[HALF - REACH :], right[:REACH]], axis=0).astype(F32)
    mid = (feat + dot(jnp.concatenate(mixed, axis=0), out_ref[...])).astype(BF16)
    beside = jnp.maximum(dot(mid, pool_ref[...]), 0.0).astype(BF16)
    count = column(own_row, 0, tokens)
    shape = (tokens, TABLE)
    ahead = iota(shape, 1) < iota(shape, 0)
    begin = atoms_before(table, me, tokens) - me * rows
    begin = begin + jnp.sum(jnp.where(ahead, own_row, 0), axis=1, keepdims=True)
    atom = iota((tokens, rows), 1)
    chosen = (atom >= begin) & (atom < begin + count)
    pooled = dot(jnp.where(chosen, 1.0, 0.0).astype(BF16), lifted_ref[...])
    lane = iota((tokens, 2 * REACH), 1)
    atom = jnp.where(lane < REACH, lane - REACH, lane - REACH + rows)
    chosen = (atom >= begin) & (atom < begin + count)
    pooled = pooled + dot(jnp.where(chosen, 1.0, 0.0).astype(BF16), beside)
    kind = column(own_row, 2 * tokens, tokens)
    onehot = jnp.where(iota((tokens, RESTYPES), 1) == kind, 1.0, 0.0).astype(BF16)
    state = single_ref[...].astype(F32) + pooled / count.astype(F32)
    state = state + dot(onehot, restype_ref[...])
    state_ref[...] = state
    token_normed = norm(state, gain_ref[...]).astype(BF16)
    for i in range(normed_ref.shape[0]):
        normed_ref[i] = token_normed


def query_kernel(
    normed_ref, table_ref, bias_ref, chain_weight_ref, proj_ref,
    query_ref, gate_ref, biased_ref, pick_ref, wv_ref,
    sem,
):
    copy = pltpu.make_async_copy(proj_ref.at[:, pl.ds(2 * CS, CS)], wv_ref, sem)
    copy.start()
    me = lax.axis_index("row")
    normed = normed_ref[0]
    tokens = normed.shape[0]
    query = dot(normed, proj_ref[:, :CS]).astype(BF16).astype(F32)
    head = iota((HEADS, CS), 1) // HDIM == iota((HEADS, CS), 0)
    spread = jnp.concatenate(
        [
            jnp.where(head, jnp.broadcast_to(query[t : t + 1], (HEADS, CS)), 0.0)
            for t in range(tokens)
        ],
        axis=0,
    ).astype(BF16)
    query_ref[...] = dot_nt(spread, proj_ref[:, CS : 2 * CS]).astype(BF16)
    table = table_ref[...]
    n = table.shape[0]
    keys = n * tokens
    shape = (TABLE, keys)
    pick = jnp.where(iota(shape, 0) == tokens + iota(shape, 1) % tokens, 1.0, 0.0).astype(BF16)
    each = dot(table.astype(F32).astype(BF16), pick)
    shape = (n, keys)
    chain_keys = jnp.sum(
        jnp.where(iota(shape, 1) // tokens == iota(shape, 0), each, 0.0), axis=0, keepdims=True
    )
    own_row = table_row(table, me)
    shape = (tokens * HEADS, TABLE)
    mine = iota(shape, 1) == tokens + iota(shape, 0) // HEADS
    chain_rows = jnp.sum(jnp.where(mine, own_row, 0), axis=1, keepdims=True).astype(F32)
    shape = (tokens * HEADS, HEADS)
    mine = iota(shape, 1) == iota(shape, 0) % HEADS
    weight = jnp.sum(jnp.where(mine, chain_weight_ref[...], 0.0), axis=1, keepdims=True)
    biased_ref[...] = bias_ref[...] + jnp.where(chain_rows == chain_keys, weight, 0.0)
    rows = pick_ref.shape[0]
    counts = jnp.where(iota(table.shape, 1) < tokens, table, 0).astype(F32).astype(BF16)
    begin = jnp.zeros((1, TABLE), F32)
    size = jnp.zeros((1, TABLE), F32)
    for step in range(3):
        shape = (TABLE, TABLE)
        token = iota(shape, 1) - step * tokens
        here = (token >= 0) & (token < tokens)
        ahead = jnp.where(here & (iota(shape, 0) < token), 1.0, 0.0).astype(BF16)
        equal = jnp.where(here & (iota(shape, 0) == token), 1.0, 0.0).astype(BF16)
        at = iota(table.shape, 0) == me + step - 1
        begin += jnp.sum(jnp.where(at, dot(counts, ahead), 0.0), axis=0, keepdims=True)
        size += jnp.sum(jnp.where(at, dot(counts, equal), 0.0), axis=0, keepdims=True)
        before = atoms_before(table, me + step - 1, tokens).astype(F32)
        begin += jnp.where(here[:1], before, 0.0)
    atom = (iota((rows, TABLE), 0) + me * rows).astype(F32)
    pick_ref[...] = jnp.where((atom >= begin) & (atom < begin + size), 1.0, 0.0).astype(BF16)
    gate_ref[...] = jax.nn.sigmoid(dot(normed, proj_ref[:, 3 * CS :]))
    copy.wait()


def attend_kernel(
    mine_ref, other_ref, query_ref, biased_ref, gate_ref, state_ref, wv_ref, out_ref, tokens_ref
):
    even = lax.rem(lax.axis_index("row"), 2) == 0
    tokens = state_ref.shape[0]
    chips = mine_ref.shape[0]
    mine, other = mine_ref[...], other_ref[...]
    first = jnp.where(even, mine, other)
    second = jnp.where(even, other, mine)
    normed = jnp.concatenate(
        [part[c] for c in range(chips) for part in (first, second)], axis=0
    )
    scores = dot_nt(query_ref[...], normed) * (1.0 / math.sqrt(HDIM)) + biased_ref[...]
    weights = jnp.exp(scores - jnp.max(scores, axis=-1, keepdims=True))
    denom = jnp.sum(weights, axis=-1, keepdims=True)
    values = dot(normed, wv_ref[...]).astype(BF16)
    mixed = dot(weights.astype(BF16), values) / denom
    head = iota((HEADS, CS), 1) // HDIM == iota((HEADS, CS), 0)
    mixed = jnp.concatenate(
        [
            jnp.sum(
                jnp.where(head, mixed[t * HEADS : (t + 1) * HEADS], 0.0), axis=0, keepdims=True
            )
            for t in range(tokens)
        ],
        axis=0,
    )
    gated = (mixed * gate_ref[...]).astype(BF16)
    tokens_ref[...] = (state_ref[...] + dot(gated, out_ref[...])).astype(BF16)


def own_kernel(mid_ref, own_ref, pick_ref, weight_ref, back_ref, partial_ref, tokens_ref):
    own = own_ref[...]
    tokens_ref[...] = own
    back = dot(own, weight_ref[...]).astype(BF16)
    back_ref[...] = back
    count = back.shape[0]
    rest = jnp.zeros((TABLE - 2 * count, CA), BF16)
    spread = dot(pick_ref[...], jnp.concatenate([jnp.zeros_like(back), back, rest], axis=0))
    partial_ref[...] = mid_ref[...].astype(F32) + spread


def beside_kernel(partial_ref, core_ref, far_ref, pick_ref, weight_ref, atoms_ref):
    even = lax.rem(lax.axis_index("row"), 2) == 0
    core, far = core_ref[...], dot(far_ref[...], weight_ref[...]).astype(BF16)
    parts = [jnp.where(even, far, core), jnp.zeros_like(core), jnp.where(even, core, far)]
    rest = jnp.zeros((TABLE - 3 * core.shape[0], CA), BF16)
    spread = dot(pick_ref[...], jnp.concatenate([*parts, rest], axis=0))
    atoms_ref[...] = (partial_ref[...] + spread).astype(BF16)


def call(kernel, outs, *args, scratch=(), aliases=None):
    spec = pl.BlockSpec(memory_space=pltpu.VMEM)
    return pl.pallas_call(
        kernel,
        out_shape=outs,
        in_specs=[spec] * len(args),
        out_specs=jax.tree.map(lambda _: spec, outs),
        scratch_shapes=list(scratch),
        input_output_aliases=aliases or {},
        compiler_params=pltpu.CompilerParams(vmem_limit_bytes=VMEM_LIMIT),
        cost_estimate=pl.CostEstimate(flops=COST, bytes_accessed=COST // 200, transcendentals=0),
    )(*args)


def shape_of(shape, dtype):
    return jax.ShapeDtypeStruct(shape, dtype)


def shards(
    atom_feat,
    window_start,
    atom_count,
    residue_type,
    chain_id,
    token_single,
    pair,
    atom_gain,
    atom_qkv,
    atom_out,
    pool_weight,
    restype_table,
    token_gain,
    token_proj,
    token_out,
    pair_gain,
    pair_bias_weight,
    chain_weight,
    back_weight,
):
    n = lax.axis_size("row")
    rows, tokens, extent = atom_feat.shape[0], token_single.shape[0], pair.shape[1]
    cores = [(i, i ^ 1) for i in range(n)]
    far = [(i, i + 1) for i in range(1, n - 1, 2)] + [(i + 1, i) for i in range(1, n - 1, 2)]
    same_core = [[2 * c + core for c in range(n // 2)] for core in range(2)]

    feat_far = lax.ppermute(atom_feat, "row", far)
    feat_core = lax.ppermute(atom_feat, "row", cores)
    table = call(
        table_kernel,
        shape_of((n, 1, TABLE), jnp.int32),
        call(first_kernel, shape_of((8, TABLE), jnp.int32)),
        atom_count[None],
        chain_id[None],
        residue_type[None],
        window_start[None],
    )
    table = lax.all_to_all(table, "row", 0, 0, tiled=True).reshape(n, TABLE)

    bias = call(
        pair_kernel, shape_of((tokens * HEADS, extent), F32), pair, pair_gain, pair_bias_weight.T
    )
    values, scores, mid, lifted = call(
        functools.partial(atom_kernel, n),
        (
            shape_of((rows + 2 * HALF, CA), BF16),
            shape_of((2, AHEADS * REACH, 2 * HALF), F32),
            shape_of((rows, CA), BF16),
            shape_of((rows, CS), BF16),
        ),
        atom_feat,
        feat_core,
        feat_far,
        window_start[None],
        atom_gain,
        atom_qkv,
        atom_out,
        pool_weight,
        bias,
    )
    state, normed = call(
        functools.partial(state_kernel, n),
        (shape_of((tokens, CS), F32), shape_of((n // 2, tokens, CS), BF16)),
        values,
        scores,
        lifted,
        feat_core,
        feat_far,
        table,
        token_single,
        atom_out,
        pool_weight,
        restype_table,
        token_gain,
    )
    mine = lax.all_to_all(normed, "row", 0, 0, tiled=True, axis_index_groups=same_core)
    query, gate, biased, pick, wv = call(
        query_kernel,
        (
            shape_of((tokens * HEADS, CS), BF16),
            shape_of((tokens, CS), F32),
            shape_of((tokens * HEADS, extent), F32),
            shape_of((rows, TABLE), BF16),
            shape_of((CS, CS), BF16),
        ),
        normed,
        table,
        bias,
        chain_weight,
        token_proj,
        scratch=(pltpu.SemaphoreType.DMA,),
        aliases={2: 2},
    )
    mine, query = lax.optimization_barrier((mine, query))
    other = lax.ppermute(mine, "row", cores)
    updated = call(
        attend_kernel,
        shape_of((tokens, CS), BF16),
        mine,
        other,
        query,
        biased,
        gate,
        state,
        wv,
        token_out,
    )
    tokens_far = lax.ppermute(updated, "row", far)
    back, partial, tokens_out = call(
        own_kernel,
        (shape_of((tokens, CA), BF16), shape_of((rows, CA), F32), shape_of((tokens, CS), BF16)),
        mid,
        updated,
        pick,
        back_weight,
    )
    back_core = lax.ppermute(back, "row", cores)
    atoms_out = call(
        beside_kernel,
        shape_of((rows, CA), BF16),
        partial,
        back_core,
        tokens_far,
        pick,
        back_weight,
    )
    return (atoms_out, tokens_out)


def solution(mesh):
    split = P(("groups", "row"), None)
    line = P(("groups", "row"))
    return jax.shard_map(
        shards,
        mesh=mesh,
        in_specs=(split, line, line, line, line, split, P(("groups", "row"), None, None))
        + (P(),) * 12,
        out_specs=(split, split),
        check_vma=False,
    )
```

```python
import functools
import math

import jax
import jax.numpy as jnp
from jax import lax
from jax.experimental import pallas as pl
from jax.experimental.pallas import tpu as pltpu
from jax.sharding import PartitionSpec as P

CA = 128
CS = 768
HEADS = 16
AHEADS = 4
RESTYPES = 32
QBLK = 32
KWIN = 128
HDIM = 48
ADIM = 32
HALF = 128
REACH = 64
VMEM_LIMIT = 24 * 1024 * 1024
COST = 2_000_000_000
EPS = 1e-05
NEG = -1e30
F32 = jnp.float32
BF16 = jnp.bfloat16
TABLE = 128


def dot(a, b):
    return lax.dot_general(a, b, (((1,), (0,)), ((), ())), preferred_element_type=F32)


def dot_nt(a, b):
    return lax.dot_general(a, b, (((1,), (1,)), ((), ())), preferred_element_type=F32)


def norm(x, gain):
    centered = x - jnp.mean(x, axis=-1, keepdims=True)
    variance = jnp.mean(centered * centered, axis=-1, keepdims=True)
    return centered * lax.rsqrt(variance + EPS) * gain


def iota(shape, axis):
    return lax.broadcasted_iota(jnp.int32, shape, axis)


def owner(shape):
    return shape[0] - 1 - iota(shape, 0)


def table_row(table, device):
    return jnp.sum(jnp.where(owner(table.shape) == device, table, 0), axis=0, keepdims=True)


def column(row, base, size):
    shape = (size, row.shape[1])
    return jnp.sum(jnp.where(iota(shape, 1) == iota(shape, 0) + base, row, 0), axis=1, keepdims=True)


def atoms_before(table, device, tokens):
    keep = (owner(table.shape) < device) & (iota(table.shape, 1) < tokens)
    return jnp.sum(jnp.sum(jnp.where(keep, table, 0), axis=0, keepdims=True), axis=1, keepdims=True)


def first_kernel(out_ref):
    out_ref[...] = jnp.zeros_like(out_ref)


def table_kernel(zero_ref, count_ref, chain_ref, kind_ref, window_ref, table_ref):
    row = zero_ref[:1]
    pieces = (count_ref, chain_ref, kind_ref, window_ref)
    base = 0
    for ref in pieces:
        size = ref.shape[1]
        shape = (size, TABLE)
        at = iota(shape, 1) == iota(shape, 0) + base
        eye = iota((size, size), 0) == iota((size, size), 1)
        values = jnp.sum(jnp.where(eye, ref[...], 0), axis=1, keepdims=True)
        row = row + jnp.sum(jnp.where(at, values, 0), axis=0, keepdims=True)
        base += size
    table_ref[...] = jnp.broadcast_to(row[None], table_ref.shape)


def pair_kernel(pair_ref, gain_ref, weight_ref, bias_ref):
    gain, weight = gain_ref[...], weight_ref[...]
    for t in range(pair_ref.shape[0]):
        normed = norm(pair_ref[t].astype(F32), gain).astype(BF16)
        bias_ref[t * HEADS : (t + 1) * HEADS, :] = dot_nt(weight, normed)


def window_scores(queries, keys):
    head = iota(queries.shape, 1) // ADIM
    stacked = jnp.concatenate(
        [jnp.where(head == h, queries, jnp.zeros_like(queries)) for h in range(AHEADS)], axis=0
    )
    return dot_nt(stacked, keys) * (1.0 / math.sqrt(ADIM))


def attend_window(scores, values, start, begin, atoms):
    count, extent = scores.shape[0] // AHEADS, scores.shape[1]
    head = iota((count, CA), 1) // ADIM
    place = iota((count, extent), 1) + begin
    inside = (place >= start) & (place < start + KWIN) & (place >= 0) & (place < atoms)
    inside = jnp.concatenate([inside.astype(F32)] * AHEADS, axis=0) > 0.5
    scores = jnp.where(inside, scores, NEG)
    weights = jnp.exp(scores - jnp.max(scores, axis=-1, keepdims=True))
    denom = jnp.sum(weights, axis=-1, keepdims=True)
    mixed = dot(weights.astype(BF16), values) / denom
    total = jnp.zeros((count, CA), F32)
    for h in range(AHEADS):
        total = total + jnp.where(head == h, mixed[h * count : (h + 1) * count], 0.0)
    return total.astype(BF16)


def block_starts(row, count, first):
    shape = (count, row.shape[1])
    lane = iota(shape, 1) - first
    return jnp.sum(jnp.where(lane == iota(shape, 0) // QBLK, row, 0), axis=1, keepdims=True)


def edges(feat_core, feat_far, rows):
    even = lax.rem(lax.axis_index("row"), 2) == 0
    left = jnp.where(even, feat_far[rows - HALF :, :], feat_core[rows - HALF :, :])
    right = jnp.where(even, feat_core[:HALF, :], feat_far[:HALF, :])
    return left, right


def atom_kernel(
    n, feat_ref, core_ref, far_ref, window_ref, gain_ref, qkv_ref, out_ref, pool_ref, bias_ref,
    values_ref, scores_ref, mid_ref, lifted_ref,
):
    me = lax.axis_index("row")
    rows = feat_ref.shape[0]
    left, right = edges(core_ref[...], far_ref[...], rows)
    feat = jnp.concatenate([left, feat_ref[...], right], axis=0).astype(F32)
    proj = dot(norm(feat, gain_ref[...]).astype(BF16), qkv_ref[...]).astype(BF16)
    values_ref[...] = proj[:, 2 * CA :]
    for i, (at, base) in enumerate(((HALF - REACH, 0), (HALF + rows, rows))):
        part = window_scores(
            proj[at : at + REACH, :CA], proj[base : base + 2 * HALF, CA : 2 * CA]
        )
        scores_ref[i] = part
    for s in range(rows // HALF):
        own = slice(HALF * s, HALF * s + HALF)
        ext = slice(HALF * s + HALF, HALF * s + 2 * HALF)
        near = slice(HALF * s + HALF - REACH, HALF * s + 3 * HALF - REACH)
        mixed = attend_window(
            window_scores(proj[ext, :CA], proj[near, CA : 2 * CA]),
            proj[near, 2 * CA :],
            block_starts(window_ref[...], HALF, s * HALF // QBLK),
            me * rows + HALF * s - REACH,
            n * rows,
        )
        mid = (feat[ext] + dot(mixed, out_ref[...])).astype(BF16)
        mid_ref[own, :] = mid
        lifted_ref[own, :] = jnp.maximum(dot(mid, pool_ref[...]), 0.0).astype(BF16)


def state_kernel(
    n, values_ref, scores_ref, lifted_ref, core_ref, far_ref, table_ref, single_ref, out_ref, pool_ref, restype_ref, gain_ref,
    state_ref, normed_ref,
):
    me = lax.axis_index("row")
    rows = lifted_ref.shape[0]
    tokens = single_ref.shape[0]
    table = table_ref[...]
    own_row = table_row(table, me)
    windows = rows // QBLK
    mixed = []
    for i, (base, row, first) in enumerate(
        ((0, me - 1, windows - REACH // QBLK), (rows, me + 1, 0))
    ):
        mixed.append(
            attend_window(
                scores_ref[i],
                values_ref[base : base + 2 * HALF, :],
                block_starts(table_row(table, row), REACH, 3 * tokens + first),
                me * rows - HALF + base,
                n * rows,
            )
        )
    left, right = edges(core_ref[...], far_ref[...], rows)
    feat = jnp.concatenate([left[HALF - REACH :], right[:REACH]], axis=0).astype(F32)
    mid = (feat + dot(jnp.concatenate(mixed, axis=0), out_ref[...])).astype(BF16)
    beside = jnp.maximum(dot(mid, pool_ref[...]), 0.0).astype(BF16)
    count = column(own_row, 0, tokens)
    shape = (tokens, TABLE)
    ahead = iota(shape, 1) < iota(shape, 0)
    begin = atoms_before(table, me, tokens) - me * rows
    begin = begin + jnp.sum(jnp.where(ahead, own_row, 0), axis=1, keepdims=True)
    atom = iota((tokens, rows), 1)
    chosen = (atom >= begin) & (atom < begin + count)
    pooled = dot(jnp.where(chosen, 1.0, 0.0).astype(BF16), lifted_ref[...])
    lane = iota((tokens, 2 * REACH), 1)
    atom = jnp.where(lane < REACH, lane - REACH, lane - REACH + rows)
    chosen = (atom >= begin) & (atom < begin + count)
    pooled = pooled + dot(jnp.where(chosen, 1.0, 0.0).astype(BF16), beside)
    kind = column(own_row, 2 * tokens, tokens)
    onehot = jnp.where(iota((tokens, RESTYPES), 1) == kind, 1.0, 0.0).astype(BF16)
    state = single_ref[...].astype(F32) + pooled / count.astype(F32)
    state = state + dot(onehot, restype_ref[...])
    state_ref[...] = state
    token_normed = norm(state, gain_ref[...]).astype(BF16)
    for i in range(normed_ref.shape[0]):
        normed_ref[i] = token_normed


def query_kernel(
    normed_ref, table_ref, bias_ref, chain_weight_ref, proj_ref,
    query_ref, gate_ref, biased_ref, pick_ref, wv_ref,
    sem,
):
    copy = pltpu.make_async_copy(proj_ref.at[:, pl.ds(2 * CS, CS)], wv_ref, sem)
    copy.start()
    me = lax.axis_index("row")
    normed = normed_ref[0]
    tokens = normed.shape[0]
    query = dot(normed, proj_ref[:, :CS]).astype(BF16).astype(F32)
    head = iota((HEADS, CS), 1) // HDIM == iota((HEADS, CS), 0)
    spread = jnp.concatenate(
        [
            jnp.where(head, jnp.broadcast_to(query[t : t + 1], (HEADS, CS)), 0.0)
            for t in range(tokens)
        ],
        axis=0,
    ).astype(BF16)
    query_ref[...] = dot_nt(spread, proj_ref[:, CS : 2 * CS]).astype(BF16)
    table = table_ref[...]
    n = table.shape[0]
    keys = n * tokens
    shape = (TABLE, keys)
    pick = jnp.where(iota(shape, 0) == tokens + iota(shape, 1) % tokens, 1.0, 0.0).astype(BF16)
    each = dot(table.astype(F32).astype(BF16), pick)
    shape = (n, keys)
    chain_keys = jnp.sum(
        jnp.where(iota(shape, 1) // tokens == owner(shape), each, 0.0), axis=0, keepdims=True
    )
    own_row = table_row(table, me)
    shape = (tokens * HEADS, TABLE)
    mine = iota(shape, 1) == tokens + iota(shape, 0) // HEADS
    chain_rows = jnp.sum(jnp.where(mine, own_row, 0), axis=1, keepdims=True).astype(F32)
    shape = (tokens * HEADS, HEADS)
    mine = iota(shape, 1) == iota(shape, 0) % HEADS
    weight = jnp.sum(jnp.where(mine, chain_weight_ref[...], 0.0), axis=1, keepdims=True)
    biased_ref[...] = bias_ref[...] + jnp.where(chain_rows == chain_keys, weight, 0.0)
    rows = pick_ref.shape[0]
    counts = jnp.where(iota(table.shape, 1) < tokens, table, 0).astype(F32).astype(BF16)
    begin = jnp.zeros((1, TABLE), F32)
    size = jnp.zeros((1, TABLE), F32)
    for step in range(3):
        shape = (TABLE, TABLE)
        token = iota(shape, 1) - step * tokens
        here = (token >= 0) & (token < tokens)
        ahead = jnp.where(here & (iota(shape, 0) < token), 1.0, 0.0).astype(BF16)
        equal = jnp.where(here & (iota(shape, 0) == token), 1.0, 0.0).astype(BF16)
        at = owner(table.shape) == me + step - 1
        begin += jnp.sum(jnp.where(at, dot(counts, ahead), 0.0), axis=0, keepdims=True)
        size += jnp.sum(jnp.where(at, dot(counts, equal), 0.0), axis=0, keepdims=True)
        before = atoms_before(table, me + step - 1, tokens).astype(F32)
        begin += jnp.where(here[:1], before, 0.0)
    atom = (iota((rows, TABLE), 0) + me * rows).astype(F32)
    pick_ref[...] = jnp.where((atom >= begin) & (atom < begin + size), 1.0, 0.0).astype(BF16)
    gate_ref[...] = jax.nn.sigmoid(dot(normed, proj_ref[:, 3 * CS :]))
    copy.wait()


def attend_kernel(
    mine_ref, other_ref, query_ref, biased_ref, gate_ref, state_ref, wv_ref, out_ref, tokens_ref
):
    even = lax.rem(lax.axis_index("row"), 2) == 0
    tokens = state_ref.shape[0]
    chips = mine_ref.shape[0]
    mine, other = mine_ref[...], other_ref[...]
    first = jnp.where(even, mine, other)
    second = jnp.where(even, other, mine)
    normed = jnp.concatenate(
        [part[(c - chips // 2) % chips] for c in range(chips) for part in (first, second)], axis=0
    )
    scores = dot_nt(query_ref[...], normed) * (1.0 / math.sqrt(HDIM)) + biased_ref[...]
    weights = jnp.exp(scores - jnp.max(scores, axis=-1, keepdims=True))
    denom = jnp.sum(weights, axis=-1, keepdims=True)
    values = dot(normed, wv_ref[...]).astype(BF16)
    mixed = dot(weights.astype(BF16), values) / denom
    head = iota((HEADS, CS), 1) // HDIM == iota((HEADS, CS), 0)
    mixed = jnp.concatenate(
        [
            jnp.sum(
                jnp.where(head, mixed[t * HEADS : (t + 1) * HEADS], 0.0), axis=0, keepdims=True
            )
            for t in range(tokens)
        ],
        axis=0,
    )
    gated = (mixed * gate_ref[...]).astype(BF16)
    tokens_ref[...] = (state_ref[...] + dot(gated, out_ref[...])).astype(BF16)


def own_kernel(mid_ref, own_ref, pick_ref, weight_ref, back_ref, partial_ref, tokens_ref):
    own = own_ref[...]
    tokens_ref[...] = own
    back = dot(own, weight_ref[...]).astype(BF16)
    back_ref[...] = back
    count = back.shape[0]
    rest = jnp.zeros((TABLE - 2 * count, CA), BF16)
    spread = dot(pick_ref[...], jnp.concatenate([jnp.zeros_like(back), back, rest], axis=0))
    partial_ref[...] = mid_ref[...].astype(F32) + spread


def beside_kernel(partial_ref, core_ref, far_ref, pick_ref, weight_ref, atoms_ref):
    even = lax.rem(lax.axis_index("row"), 2) == 0
    core, far = core_ref[...], dot(far_ref[...], weight_ref[...]).astype(BF16)
    parts = [jnp.where(even, far, core), jnp.zeros_like(core), jnp.where(even, core, far)]
    rest = jnp.zeros((TABLE - 3 * core.shape[0], CA), BF16)
    spread = dot(pick_ref[...], jnp.concatenate([*parts, rest], axis=0))
    atoms_ref[...] = (partial_ref[...] + spread).astype(BF16)


def call(kernel, outs, *args, scratch=(), aliases=None):
    spec = pl.BlockSpec(memory_space=pltpu.VMEM)
    return pl.pallas_call(
        kernel,
        out_shape=outs,
        in_specs=[spec] * len(args),
        out_specs=jax.tree.map(lambda _: spec, outs),
        scratch_shapes=list(scratch),
        input_output_aliases=aliases or {},
        compiler_params=pltpu.CompilerParams(vmem_limit_bytes=VMEM_LIMIT),
        cost_estimate=pl.CostEstimate(flops=COST, bytes_accessed=COST // 200, transcendentals=0),
    )(*args)


def shape_of(shape, dtype):
    return jax.ShapeDtypeStruct(shape, dtype)


def shards(
    atom_feat,
    window_start,
    atom_count,
    residue_type,
    chain_id,
    token_single,
    pair,
    atom_gain,
    atom_qkv,
    atom_out,
    pool_weight,
    restype_table,
    token_gain,
    token_proj,
    token_out,
    pair_gain,
    pair_bias_weight,
    chain_weight,
    back_weight,
):
    n = lax.axis_size("row")
    rows, tokens, extent = atom_feat.shape[0], token_single.shape[0], pair.shape[1]
    cores = [(i, i ^ 1) for i in range(n)]
    far = [(i, i + 1) for i in range(1, n - 1, 2)] + [(i + 1, i) for i in range(1, n - 1, 2)]
    chips = n // 2
    same_core = [[2 * ((c + chips // 2) % chips) + core for c in range(chips)] for core in range(2)]
    backwards = [list(reversed(range(n)))]

    feat_far = lax.ppermute(atom_feat, "row", far)
    feat_core = lax.ppermute(atom_feat, "row", cores)
    table = call(
        table_kernel,
        shape_of((n, 1, TABLE), jnp.int32),
        call(first_kernel, shape_of((8, TABLE), jnp.int32)),
        atom_count[None],
        chain_id[None],
        residue_type[None],
        window_start[None],
    )
    table = lax.all_to_all(table, "row", 0, 0, tiled=True, axis_index_groups=backwards).reshape(n, TABLE)

    bias = call(
        pair_kernel, shape_of((tokens * HEADS, extent), F32), pair, pair_gain, pair_bias_weight.T
    )
    values, scores, mid, lifted = call(
        functools.partial(atom_kernel, n),
        (
            shape_of((rows + 2 * HALF, CA), BF16),
            shape_of((2, AHEADS * REACH, 2 * HALF), F32),
            shape_of((rows, CA), BF16),
            shape_of((rows, CS), BF16),
        ),
        atom_feat,
        feat_core,
        feat_far,
        window_start[None],
        atom_gain,
        atom_qkv,
        atom_out,
        pool_weight,
        bias,
    )
    state, normed = call(
        functools.partial(state_kernel, n),
        (shape_of((tokens, CS), F32), shape_of((n // 2, tokens, CS), BF16)),
        values,
        scores,
        lifted,
        feat_core,
        feat_far,
        table,
        token_single,
        atom_out,
        pool_weight,
        restype_table,
        token_gain,
    )
    mine = lax.all_to_all(normed, "row", 0, 0, tiled=True, axis_index_groups=same_core)
    query, gate, biased, pick, wv = call(
        query_kernel,
        (
            shape_of((tokens * HEADS, CS), BF16),
            shape_of((tokens, CS), F32),
            shape_of((tokens * HEADS, extent), F32),
            shape_of((rows, TABLE), BF16),
            shape_of((CS, CS), BF16),
        ),
        normed,
        table,
        bias,
        chain_weight,
        token_proj,
        scratch=(pltpu.SemaphoreType.DMA,),
        aliases={2: 2},
    )
    mine, query = lax.optimization_barrier((mine, query))
    other = lax.ppermute(mine, "row", cores)
    updated = call(
        attend_kernel,
        shape_of((tokens, CS), BF16),
        mine,
        other,
        query,
        biased,
        gate,
        state,
        wv,
        token_out,
    )
    tokens_far = lax.ppermute(updated, "row", far)
    back, partial, tokens_out = call(
        own_kernel,
        (shape_of((tokens, CA), BF16), shape_of((rows, CA), F32), shape_of((tokens, CS), BF16)),
        mid,
        updated,
        pick,
        back_weight,
    )
    back_core = lax.ppermute(back, "row", cores)
    atoms_out = call(
        beside_kernel,
        shape_of((rows, CA), BF16),
        partial,
        back_core,
        tokens_far,
        pick,
        back_weight,
    )
    return (atoms_out, tokens_out)


def solution(mesh):
    split = P(("groups", "row"), None)
    line = P(("groups", "row"))
    return jax.shard_map(
        shards,
        mesh=mesh,
        in_specs=(split, line, line, line, line, split, P(("groups", "row"), None, None))
        + (P(),) * 12,
        out_specs=(split, split),
        check_vma=False,
    )
```

```python
import functools
import math

import jax
import jax.numpy as jnp
from jax import lax
from jax.experimental import pallas as pl
from jax.experimental.pallas import tpu as pltpu
from jax.sharding import PartitionSpec as P

CA = 128
CS = 768
HEADS = 16
AHEADS = 4
RESTYPES = 32
QBLK = 32
KWIN = 128
HDIM = 48
ADIM = 32
HALF = 128
REACH = 64
VMEM_LIMIT = 24 * 1024 * 1024
COST = 2_000_000_000
EPS = 1e-05
NEG = -1e30
F32 = jnp.float32
BF16 = jnp.bfloat16
TABLE = 128


def dot(a, b):
    return lax.dot_general(a, b, (((1,), (0,)), ((), ())), preferred_element_type=F32)


def dot_nt(a, b):
    return lax.dot_general(a, b, (((1,), (1,)), ((), ())), preferred_element_type=F32)


def norm(x, gain):
    centered = x - jnp.mean(x, axis=-1, keepdims=True)
    variance = jnp.mean(centered * centered, axis=-1, keepdims=True)
    return centered * lax.rsqrt(variance + EPS) * gain


def iota(shape, axis):
    return lax.broadcasted_iota(jnp.int32, shape, axis)


def owner(shape):
    return shape[0] - 1 - iota(shape, 0)


def table_row(table, device):
    return jnp.sum(jnp.where(owner(table.shape) == device, table, 0), axis=0, keepdims=True)


def column(row, base, size):
    shape = (size, row.shape[1])
    return jnp.sum(jnp.where(iota(shape, 1) == iota(shape, 0) + base, row, 0), axis=1, keepdims=True)


def atoms_before(table, device, tokens):
    keep = (owner(table.shape) < device) & (iota(table.shape, 1) < tokens)
    return jnp.sum(jnp.sum(jnp.where(keep, table, 0), axis=0, keepdims=True), axis=1, keepdims=True)


def first_kernel(out_ref):
    out_ref[...] = jnp.zeros_like(out_ref)


def table_kernel(zero_ref, count_ref, chain_ref, kind_ref, window_ref, table_ref):
    row = zero_ref[:1]
    pieces = (count_ref, chain_ref, kind_ref, window_ref)
    base = 0
    for ref in pieces:
        size = ref.shape[1]
        shape = (size, TABLE)
        at = iota(shape, 1) == iota(shape, 0) + base
        eye = iota((size, size), 0) == iota((size, size), 1)
        values = jnp.sum(jnp.where(eye, ref[...], 0), axis=1, keepdims=True)
        row = row + jnp.sum(jnp.where(at, values, 0), axis=0, keepdims=True)
        base += size
    table_ref[...] = jnp.broadcast_to(row[None], table_ref.shape)


def pair_kernel(pair_ref, gain_ref, weight_ref, bias_ref):
    gain, weight = gain_ref[...], weight_ref[...]
    width = pair_ref.shape[2]
    average = jnp.full((width, width), 1.0 / width, BF16)
    for t in range(pair_ref.shape[0]):
        pair = pair_ref[t]
        centered = pair.astype(F32) - dot(pair, average)
        variance = jnp.mean(centered * centered, axis=-1, keepdims=True)
        normed = (centered * lax.rsqrt(variance + EPS) * gain).astype(BF16)
        bias_ref[t * HEADS : (t + 1) * HEADS, :] = dot_nt(weight, normed)


def window_scores(queries, keys):
    head = iota(queries.shape, 1) // ADIM
    stacked = jnp.concatenate(
        [jnp.where(head == h, queries, jnp.zeros_like(queries)) for h in range(AHEADS)], axis=0
    )
    return dot_nt(stacked, keys) * (1.0 / math.sqrt(ADIM))


def attend_window(scores, values, start, begin, atoms):
    count, extent = scores.shape[0] // AHEADS, scores.shape[1]
    head = iota((count, CA), 1) // ADIM
    place = iota((count, extent), 1) + begin
    inside = (place >= start) & (place < start + KWIN) & (place >= 0) & (place < atoms)
    inside = jnp.concatenate([inside.astype(F32)] * AHEADS, axis=0) > 0.5
    scores = jnp.where(inside, scores, NEG)
    weights = jnp.exp(scores - jnp.max(scores, axis=-1, keepdims=True))
    denom = jnp.sum(weights, axis=-1, keepdims=True)
    mixed = dot(weights.astype(BF16), values) / denom
    total = jnp.zeros((count, CA), F32)
    for h in range(AHEADS):
        total = total + jnp.where(head == h, mixed[h * count : (h + 1) * count], 0.0)
    return total.astype(BF16)


def block_starts(row, count, first):
    shape = (count, row.shape[1])
    lane = iota(shape, 1) - first
    return jnp.sum(jnp.where(lane == iota(shape, 0) // QBLK, row, 0), axis=1, keepdims=True)


def edges(feat_core, feat_far, rows):
    even = lax.rem(lax.axis_index("row"), 2) == 0
    left = jnp.where(even, feat_far[rows - HALF :, :], feat_core[rows - HALF :, :])
    right = jnp.where(even, feat_core[:HALF, :], feat_far[:HALF, :])
    return left, right


def atom_kernel(
    n, feat_ref, core_ref, far_ref, window_ref, gain_ref, qkv_ref, out_ref, pool_ref, bias_ref,
    values_ref, scores_ref, mid_ref, lifted_ref,
):
    me = lax.axis_index("row")
    rows = feat_ref.shape[0]
    left, right = edges(core_ref[...], far_ref[...], rows)
    feat = jnp.concatenate([left, feat_ref[...], right], axis=0).astype(F32)
    proj = dot(norm(feat, gain_ref[...]).astype(BF16), qkv_ref[...]).astype(BF16)
    values_ref[...] = proj[:, 2 * CA :]
    for i, (at, base) in enumerate(((HALF - REACH, 0), (HALF + rows, rows))):
        part = window_scores(
            proj[at : at + REACH, :CA], proj[base : base + 2 * HALF, CA : 2 * CA]
        )
        scores_ref[i] = part
    for s in range(rows // HALF):
        own = slice(HALF * s, HALF * s + HALF)
        ext = slice(HALF * s + HALF, HALF * s + 2 * HALF)
        near = slice(HALF * s + HALF - REACH, HALF * s + 3 * HALF - REACH)
        mixed = attend_window(
            window_scores(proj[ext, :CA], proj[near, CA : 2 * CA]),
            proj[near, 2 * CA :],
            block_starts(window_ref[...], HALF, s * HALF // QBLK),
            me * rows + HALF * s - REACH,
            n * rows,
        )
        mid = (feat[ext] + dot(mixed, out_ref[...])).astype(BF16)
        mid_ref[own, :] = mid
        lifted_ref[own, :] = jnp.maximum(dot(mid, pool_ref[...]), 0.0).astype(BF16)


def state_kernel(
    n, values_ref, scores_ref, lifted_ref, core_ref, far_ref, table_ref, single_ref, out_ref, pool_ref, restype_ref, gain_ref,
    state_ref, normed_ref,
):
    me = lax.axis_index("row")
    rows = lifted_ref.shape[0]
    tokens = single_ref.shape[0]
    table = table_ref[...]
    own_row = table_row(table, me)
    windows = rows // QBLK
    mixed = []
    for i, (base, row, first) in enumerate(
        ((0, me - 1, windows - REACH // QBLK), (rows, me + 1, 0))
    ):
        mixed.append(
            attend_window(
                scores_ref[i],
                values_ref[base : base + 2 * HALF, :],
                block_starts(table_row(table, row), REACH, 3 * tokens + first),
                me * rows - HALF + base,
                n * rows,
            )
        )
    left, right = edges(core_ref[...], far_ref[...], rows)
    feat = jnp.concatenate([left[HALF - REACH :], right[:REACH]], axis=0).astype(F32)
    mid = (feat + dot(jnp.concatenate(mixed, axis=0), out_ref[...])).astype(BF16)
    beside = jnp.maximum(dot(mid, pool_ref[...]), 0.0).astype(BF16)
    count = column(own_row, 0, tokens)
    shape = (tokens, TABLE)
    ahead = iota(shape, 1) < iota(shape, 0)
    begin = atoms_before(table, me, tokens) - me * rows
    begin = begin + jnp.sum(jnp.where(ahead, own_row, 0), axis=1, keepdims=True)
    atom = iota((tokens, rows), 1)
    chosen = (atom >= begin) & (atom < begin + count)
    pooled = dot(jnp.where(chosen, 1.0, 0.0).astype(BF16), lifted_ref[...])
    lane = iota((tokens, 2 * REACH), 1)
    atom = jnp.where(lane < REACH, lane - REACH, lane - REACH + rows)
    chosen = (atom >= begin) & (atom < begin + count)
    pooled = pooled + dot(jnp.where(chosen, 1.0, 0.0).astype(BF16), beside)
    kind = column(own_row, 2 * tokens, tokens)
    onehot = jnp.where(iota((tokens, RESTYPES), 1) == kind, 1.0, 0.0).astype(BF16)
    state = single_ref[...].astype(F32) + pooled / count.astype(F32)
    state = state + dot(onehot, restype_ref[...])
    state_ref[...] = state
    token_normed = norm(state, gain_ref[...]).astype(BF16)
    for i in range(normed_ref.shape[0]):
        normed_ref[i] = token_normed


def query_kernel(
    normed_ref, table_ref, bias_ref, chain_weight_ref, proj_ref,
    query_ref, gate_ref, biased_ref, pick_ref, wv_ref,
    sem,
):
    copy = pltpu.make_async_copy(proj_ref.at[:, pl.ds(2 * CS, CS)], wv_ref, sem)
    copy.start()
    me = lax.axis_index("row")
    normed = normed_ref[0]
    tokens = normed.shape[0]
    query = dot(normed, proj_ref[:, :CS]).astype(BF16).astype(F32)
    head = iota((HEADS, CS), 1) // HDIM == iota((HEADS, CS), 0)
    spread = jnp.concatenate(
        [
            jnp.where(head, jnp.broadcast_to(query[t : t + 1], (HEADS, CS)), 0.0)
            for t in range(tokens)
        ],
        axis=0,
    ).astype(BF16)
    query_ref[...] = dot_nt(spread, proj_ref[:, CS : 2 * CS]).astype(BF16)
    table = table_ref[...]
    n = table.shape[0]
    keys = n * tokens
    shape = (TABLE, keys)
    pick = jnp.where(iota(shape, 0) == tokens + iota(shape, 1) % tokens, 1.0, 0.0).astype(BF16)
    each = dot(table.astype(F32).astype(BF16), pick)
    shape = (n, keys)
    chain_keys = jnp.sum(
        jnp.where(iota(shape, 1) // tokens == owner(shape), each, 0.0), axis=0, keepdims=True
    )
    own_row = table_row(table, me)
    shape = (tokens * HEADS, TABLE)
    mine = iota(shape, 1) == tokens + iota(shape, 0) // HEADS
    chain_rows = jnp.sum(jnp.where(mine, own_row, 0), axis=1, keepdims=True).astype(F32)
    shape = (tokens * HEADS, HEADS)
    mine = iota(shape, 1) == iota(shape, 0) % HEADS
    weight = jnp.sum(jnp.where(mine, chain_weight_ref[...], 0.0), axis=1, keepdims=True)
    biased_ref[...] = bias_ref[...] + jnp.where(chain_rows == chain_keys, weight, 0.0)
    rows = pick_ref.shape[0]
    counts = jnp.where(iota(table.shape, 1) < tokens, table, 0).astype(F32).astype(BF16)
    begin = jnp.zeros((1, TABLE), F32)
    size = jnp.zeros((1, TABLE), F32)
    for step in range(3):
        shape = (TABLE, TABLE)
        token = iota(shape, 1) - step * tokens
        here = (token >= 0) & (token < tokens)
        ahead = jnp.where(here & (iota(shape, 0) < token), 1.0, 0.0).astype(BF16)
        equal = jnp.where(here & (iota(shape, 0) == token), 1.0, 0.0).astype(BF16)
        at = owner(table.shape) == me + step - 1
        begin += jnp.sum(jnp.where(at, dot(counts, ahead), 0.0), axis=0, keepdims=True)
        size += jnp.sum(jnp.where(at, dot(counts, equal), 0.0), axis=0, keepdims=True)
        before = atoms_before(table, me + step - 1, tokens).astype(F32)
        begin += jnp.where(here[:1], before, 0.0)
    atom = (iota((rows, TABLE), 0) + me * rows).astype(F32)
    pick_ref[...] = jnp.where((atom >= begin) & (atom < begin + size), 1.0, 0.0).astype(BF16)
    gate_ref[...] = jax.nn.sigmoid(dot(normed, proj_ref[:, 3 * CS :]))
    copy.wait()


def attend_kernel(
    mine_ref, other_ref, query_ref, biased_ref, gate_ref, state_ref, wv_ref, out_ref, tokens_ref
):
    even = lax.rem(lax.axis_index("row"), 2) == 0
    tokens = state_ref.shape[0]
    chips = mine_ref.shape[0]
    mine, other = mine_ref[...], other_ref[...]
    first = jnp.where(even, mine, other)
    second = jnp.where(even, other, mine)
    normed = jnp.concatenate(
        [part[(c - chips // 2) % chips] for c in range(chips) for part in (first, second)], axis=0
    )
    scores = dot_nt(query_ref[...], normed) * (1.0 / math.sqrt(HDIM)) + biased_ref[...]
    weights = jnp.exp(scores - jnp.max(scores, axis=-1, keepdims=True))
    denom = jnp.sum(weights, axis=-1, keepdims=True)
    values = dot(normed, wv_ref[...]).astype(BF16)
    mixed = dot(weights.astype(BF16), values) / denom
    head = iota((HEADS, CS), 1) // HDIM == iota((HEADS, CS), 0)
    mixed = jnp.concatenate(
        [
            jnp.sum(
                jnp.where(head, mixed[t * HEADS : (t + 1) * HEADS], 0.0), axis=0, keepdims=True
            )
            for t in range(tokens)
        ],
        axis=0,
    )
    gated = (mixed * gate_ref[...]).astype(BF16)
    tokens_ref[...] = (state_ref[...] + dot(gated, out_ref[...])).astype(BF16)


def own_kernel(mid_ref, own_ref, pick_ref, weight_ref, back_ref, partial_ref, tokens_ref):
    own = own_ref[...]
    tokens_ref[...] = own
    back = dot(own, weight_ref[...]).astype(BF16)
    back_ref[...] = back
    count = back.shape[0]
    rest = jnp.zeros((TABLE - 2 * count, CA), BF16)
    spread = dot(pick_ref[...], jnp.concatenate([jnp.zeros_like(back), back, rest], axis=0))
    partial_ref[...] = mid_ref[...].astype(F32) + spread


def beside_kernel(partial_ref, core_ref, far_ref, pick_ref, weight_ref, atoms_ref):
    even = lax.rem(lax.axis_index("row"), 2) == 0
    core, far = core_ref[...], dot(far_ref[...], weight_ref[...]).astype(BF16)
    parts = [jnp.where(even, far, core), jnp.zeros_like(core), jnp.where(even, core, far)]
    rest = jnp.zeros((TABLE - 3 * core.shape[0], CA), BF16)
    spread = dot(pick_ref[...], jnp.concatenate([*parts, rest], axis=0))
    atoms_ref[...] = (partial_ref[...] + spread).astype(BF16)


def call(kernel, outs, *args, scratch=(), aliases=None):
    spec = pl.BlockSpec(memory_space=pltpu.VMEM)
    return pl.pallas_call(
        kernel,
        out_shape=outs,
        in_specs=[spec] * len(args),
        out_specs=jax.tree.map(lambda _: spec, outs),
        scratch_shapes=list(scratch),
        input_output_aliases=aliases or {},
        compiler_params=pltpu.CompilerParams(vmem_limit_bytes=VMEM_LIMIT),
        cost_estimate=pl.CostEstimate(flops=COST, bytes_accessed=COST // 200, transcendentals=0),
    )(*args)


def shape_of(shape, dtype):
    return jax.ShapeDtypeStruct(shape, dtype)


def shards(
    atom_feat,
    window_start,
    atom_count,
    residue_type,
    chain_id,
    token_single,
    pair,
    atom_gain,
    atom_qkv,
    atom_out,
    pool_weight,
    restype_table,
    token_gain,
    token_proj,
    token_out,
    pair_gain,
    pair_bias_weight,
    chain_weight,
    back_weight,
):
    n = lax.axis_size("row")
    rows, tokens, extent = atom_feat.shape[0], token_single.shape[0], pair.shape[1]
    cores = [(i, i ^ 1) for i in range(n)]
    far = [(i, i + 1) for i in range(1, n - 1, 2)] + [(i + 1, i) for i in range(1, n - 1, 2)]
    chips = n // 2
    same_core = [[2 * ((c + chips // 2) % chips) + core for c in range(chips)] for core in range(2)]
    backwards = [list(reversed(range(n)))]

    feat_far = lax.ppermute(atom_feat, "row", far)
    feat_core = lax.ppermute(atom_feat, "row", cores)
    table = call(
        table_kernel,
        shape_of((n, 1, TABLE), jnp.int32),
        call(first_kernel, shape_of((8, TABLE), jnp.int32)),
        atom_count[None],
        chain_id[None],
        residue_type[None],
        window_start[None],
    )
    table = lax.all_to_all(table, "row", 0, 0, tiled=True, axis_index_groups=backwards).reshape(n, TABLE)

    bias = call(
        pair_kernel, shape_of((tokens * HEADS, extent), F32), pair, pair_gain, pair_bias_weight.T
    )
    values, scores, mid, lifted = call(
        functools.partial(atom_kernel, n),
        (
            shape_of((rows + 2 * HALF, CA), BF16),
            shape_of((2, AHEADS * REACH, 2 * HALF), F32),
            shape_of((rows, CA), BF16),
            shape_of((rows, CS), BF16),
        ),
        atom_feat,
        feat_core,
        feat_far,
        window_start[None],
        atom_gain,
        atom_qkv,
        atom_out,
        pool_weight,
        bias,
    )
    state, normed = call(
        functools.partial(state_kernel, n),
        (shape_of((tokens, CS), F32), shape_of((n // 2, tokens, CS), BF16)),
        values,
        scores,
        lifted,
        feat_core,
        feat_far,
        table,
        token_single,
        atom_out,
        pool_weight,
        restype_table,
        token_gain,
    )
    mine = lax.all_to_all(normed, "row", 0, 0, tiled=True, axis_index_groups=same_core)
    query, gate, biased, pick, wv = call(
        query_kernel,
        (
            shape_of((tokens * HEADS, CS), BF16),
            shape_of((tokens, CS), F32),
            shape_of((tokens * HEADS, extent), F32),
            shape_of((rows, TABLE), BF16),
            shape_of((CS, CS), BF16),
        ),
        normed,
        table,
        bias,
        chain_weight,
        token_proj,
        scratch=(pltpu.SemaphoreType.DMA,),
        aliases={2: 2},
    )
    mine, query = lax.optimization_barrier((mine, query))
    other = lax.ppermute(mine, "row", cores)
    updated = call(
        attend_kernel,
        shape_of((tokens, CS), BF16),
        mine,
        other,
        query,
        biased,
        gate,
        state,
        wv,
        token_out,
    )
    tokens_far = lax.ppermute(updated, "row", far)
    back, partial, tokens_out = call(
        own_kernel,
        (shape_of((tokens, CA), BF16), shape_of((rows, CA), F32), shape_of((tokens, CS), BF16)),
        mid,
        updated,
        pick,
        back_weight,
    )
    back_core = lax.ppermute(back, "row", cores)
    atoms_out = call(
        beside_kernel,
        shape_of((rows, CA), BF16),
        partial,
        back_core,
        tokens_far,
        pick,
        back_weight,
    )
    return (atoms_out, tokens_out)


def solution(mesh):
    split = P(("groups", "row"), None)
    line = P(("groups", "row"))
    return jax.shard_map(
        shards,
        mesh=mesh,
        in_specs=(split, line, line, line, line, split, P(("groups", "row"), None, None))
        + (P(),) * 12,
        out_specs=(split, split),
        check_vma=False,
    )
```

```python
import functools
import math

import jax
import jax.numpy as jnp
from jax import lax
from jax.experimental import pallas as pl
from jax.experimental.pallas import tpu as pltpu
from jax.sharding import PartitionSpec as P

CA = 128
CS = 768
HEADS = 16
AHEADS = 4
RESTYPES = 32
QBLK = 32
KWIN = 128
HDIM = 48
ADIM = 32
HALF = 128
REACH = 64
VMEM_LIMIT = 24 * 1024 * 1024
COST = 2_000_000_000
EPS = 1e-05
NEG = -1e30
F32 = jnp.float32
BF16 = jnp.bfloat16
TABLE = 128


def dot(a, b):
    return lax.dot_general(a, b, (((1,), (0,)), ((), ())), preferred_element_type=F32)


def dot_nt(a, b):
    return lax.dot_general(a, b, (((1,), (1,)), ((), ())), preferred_element_type=F32)


def norm(x, gain):
    centered = x - jnp.mean(x, axis=-1, keepdims=True)
    variance = jnp.mean(centered * centered, axis=-1, keepdims=True)
    return centered * lax.rsqrt(variance + EPS) * gain


def iota(shape, axis):
    return lax.broadcasted_iota(jnp.int32, shape, axis)


def owner(shape):
    return shape[0] - 1 - iota(shape, 0)


def table_row(table, device):
    return jnp.sum(jnp.where(owner(table.shape) == device, table, 0), axis=0, keepdims=True)


def column(row, base, size):
    shape = (size, row.shape[1])
    return jnp.sum(jnp.where(iota(shape, 1) == iota(shape, 0) + base, row, 0), axis=1, keepdims=True)


def atoms_before(table, device, tokens):
    keep = (owner(table.shape) < device) & (iota(table.shape, 1) < tokens)
    return jnp.sum(jnp.sum(jnp.where(keep, table, 0), axis=0, keepdims=True), axis=1, keepdims=True)


def first_kernel(out_ref):
    out_ref[...] = jnp.zeros_like(out_ref)


def table_kernel(zero_ref, count_ref, chain_ref, kind_ref, window_ref, table_ref):
    row = zero_ref[:1]
    pieces = (count_ref, chain_ref, kind_ref, window_ref)
    base = 0
    for ref in pieces:
        size = ref.shape[1]
        shape = (size, TABLE)
        at = iota(shape, 1) == iota(shape, 0) + base
        eye = iota((size, size), 0) == iota((size, size), 1)
        values = jnp.sum(jnp.where(eye, ref[...], 0), axis=1, keepdims=True)
        row = row + jnp.sum(jnp.where(at, values, 0), axis=0, keepdims=True)
        base += size
    table_ref[...] = jnp.broadcast_to(row[None], table_ref.shape)


def pair_kernel(pair_ref, gain_ref, weight_ref, bias_ref):
    gain, weight = gain_ref[...], weight_ref[...]
    width = pair_ref.shape[2]
    average = jnp.full((width, width), 1.0 / width, BF16)
    for t in range(pair_ref.shape[0]):
        pair = pair_ref[t]
        centered = pair.astype(F32) - dot(pair, average)
        variance = jnp.mean(centered * centered, axis=-1, keepdims=True)
        normed = (centered * lax.rsqrt(variance + EPS) * gain).astype(BF16)
        bias_ref[t * HEADS : (t + 1) * HEADS, :] = dot_nt(weight, normed)


def window_scores(queries, keys):
    head = iota(queries.shape, 1) // ADIM
    stacked = jnp.concatenate(
        [jnp.where(head == h, queries, jnp.zeros_like(queries)) for h in range(AHEADS)], axis=0
    )
    return dot_nt(stacked, keys) * (1.0 / math.sqrt(ADIM))


def attend_window(scores, values, start, begin, atoms):
    count, extent = scores.shape[0] // AHEADS, scores.shape[1]
    head = iota((count, CA), 1) // ADIM
    place = iota((count, extent), 1) + begin
    inside = (place >= start) & (place < start + KWIN) & (place >= 0) & (place < atoms)
    inside = jnp.concatenate([inside.astype(F32)] * AHEADS, axis=0) > 0.5
    scores = jnp.where(inside, scores, NEG)
    weights = jnp.exp(scores - jnp.max(scores, axis=-1, keepdims=True))
    denom = jnp.sum(weights, axis=-1, keepdims=True)
    mixed = dot(weights.astype(BF16), values) / denom
    total = jnp.zeros((count, CA), F32)
    for h in range(AHEADS):
        total = total + jnp.where(head == h, mixed[h * count : (h + 1) * count], 0.0)
    return total.astype(BF16)


def block_starts(row, count, first):
    shape = (count, row.shape[1])
    lane = iota(shape, 1) - first
    return jnp.sum(jnp.where(lane == iota(shape, 0) // QBLK, row, 0), axis=1, keepdims=True)


def edges(feat_core, feat_far, rows):
    even = lax.rem(lax.axis_index("row"), 2) == 0
    left = jnp.where(even, feat_far[rows - HALF :, :], feat_core[rows - HALF :, :])
    right = jnp.where(even, feat_core[:HALF, :], feat_far[:HALF, :])
    return left, right


def atom_kernel(
    n, feat_ref, core_ref, far_ref, window_ref, gain_ref, qkv_ref, out_ref, pool_ref, bias_ref,
    values_ref, scores_ref, mid_ref, lifted_ref,
):
    me = lax.axis_index("row")
    rows = feat_ref.shape[0]
    left, right = edges(core_ref[...], far_ref[...], rows)
    feat = jnp.concatenate([left, feat_ref[...], right], axis=0)
    centered = feat.astype(F32) - dot(feat, jnp.full((CA, CA), 1.0 / CA, BF16))
    variance = jnp.mean(centered * centered, axis=-1, keepdims=True)
    normed = (centered * lax.rsqrt(variance + EPS) * gain_ref[...]).astype(BF16)
    feat = feat.astype(F32)
    proj = dot(normed, qkv_ref[...]).astype(BF16)
    values_ref[...] = proj[:, 2 * CA :]
    for i, (at, base) in enumerate(((HALF - REACH, 0), (HALF + rows, rows))):
        part = window_scores(
            proj[at : at + REACH, :CA], proj[base : base + 2 * HALF, CA : 2 * CA]
        )
        scores_ref[i] = part
    for s in range(rows // HALF):
        own = slice(HALF * s, HALF * s + HALF)
        ext = slice(HALF * s + HALF, HALF * s + 2 * HALF)
        near = slice(HALF * s + HALF - REACH, HALF * s + 3 * HALF - REACH)
        mixed = attend_window(
            window_scores(proj[ext, :CA], proj[near, CA : 2 * CA]),
            proj[near, 2 * CA :],
            block_starts(window_ref[...], HALF, s * HALF // QBLK),
            me * rows + HALF * s - REACH,
            n * rows,
        )
        mid = (feat[ext] + dot(mixed, out_ref[...])).astype(BF16)
        mid_ref[own, :] = mid
        lifted_ref[own, :] = jnp.maximum(dot(mid, pool_ref[...]), 0.0).astype(BF16)


def state_kernel(
    n, values_ref, scores_ref, lifted_ref, core_ref, far_ref, table_ref, single_ref, out_ref, pool_ref, restype_ref, gain_ref,
    state_ref, normed_ref,
):
    me = lax.axis_index("row")
    rows = lifted_ref.shape[0]
    tokens = single_ref.shape[0]
    table = table_ref[...]
    own_row = table_row(table, me)
    windows = rows // QBLK
    mixed = []
    for i, (base, row, first) in enumerate(
        ((0, me - 1, windows - REACH // QBLK), (rows, me + 1, 0))
    ):
        mixed.append(
            attend_window(
                scores_ref[i],
                values_ref[base : base + 2 * HALF, :],
                block_starts(table_row(table, row), REACH, 3 * tokens + first),
                me * rows - HALF + base,
                n * rows,
            )
        )
    left, right = edges(core_ref[...], far_ref[...], rows)
    feat = jnp.concatenate([left[HALF - REACH :], right[:REACH]], axis=0).astype(F32)
    mid = (feat + dot(jnp.concatenate(mixed, axis=0), out_ref[...])).astype(BF16)
    beside = jnp.maximum(dot(mid, pool_ref[...]), 0.0).astype(BF16)
    count = column(own_row, 0, tokens)
    shape = (tokens, TABLE)
    ahead = iota(shape, 1) < iota(shape, 0)
    begin = atoms_before(table, me, tokens) - me * rows
    begin = begin + jnp.sum(jnp.where(ahead, own_row, 0), axis=1, keepdims=True)
    atom = iota((tokens, rows), 1)
    chosen = (atom >= begin) & (atom < begin + count)
    pooled = dot(jnp.where(chosen, 1.0, 0.0).astype(BF16), lifted_ref[...])
    lane = iota((tokens, 2 * REACH), 1)
    atom = jnp.where(lane < REACH, lane - REACH, lane - REACH + rows)
    chosen = (atom >= begin) & (atom < begin + count)
    pooled = pooled + dot(jnp.where(chosen, 1.0, 0.0).astype(BF16), beside)
    kind = column(own_row, 2 * tokens, tokens)
    onehot = jnp.where(iota((tokens, RESTYPES), 1) == kind, 1.0, 0.0).astype(BF16)
    state = single_ref[...].astype(F32) + pooled / count.astype(F32)
    state = state + dot(onehot, restype_ref[...])
    state_ref[...] = state
    token_normed = norm(state, gain_ref[...]).astype(BF16)
    for i in range(normed_ref.shape[0]):
        normed_ref[i] = token_normed


def query_kernel(
    normed_ref, table_ref, bias_ref, chain_weight_ref, proj_ref,
    query_ref, gate_ref, biased_ref, pick_ref, wv_ref,
    sem,
):
    copy = pltpu.make_async_copy(proj_ref.at[:, pl.ds(2 * CS, CS)], wv_ref, sem)
    copy.start()
    me = lax.axis_index("row")
    normed = normed_ref[0]
    tokens = normed.shape[0]
    query = dot(normed, proj_ref[:, :CS]).astype(BF16).astype(F32)
    head = iota((HEADS, CS), 1) // HDIM == iota((HEADS, CS), 0)
    spread = jnp.concatenate(
        [
            jnp.where(head, jnp.broadcast_to(query[t : t + 1], (HEADS, CS)), 0.0)
            for t in range(tokens)
        ],
        axis=0,
    ).astype(BF16)
    query_ref[...] = dot_nt(spread, proj_ref[:, CS : 2 * CS]).astype(BF16)
    table = table_ref[...]
    n = table.shape[0]
    keys = n * tokens
    shape = (TABLE, keys)
    pick = jnp.where(iota(shape, 0) == tokens + iota(shape, 1) % tokens, 1.0, 0.0).astype(BF16)
    each = dot(table.astype(F32).astype(BF16), pick)
    shape = (n, keys)
    chain_keys = jnp.sum(
        jnp.where(iota(shape, 1) // tokens == owner(shape), each, 0.0), axis=0, keepdims=True
    )
    own_row = table_row(table, me)
    shape = (tokens * HEADS, TABLE)
    mine = iota(shape, 1) == tokens + iota(shape, 0) // HEADS
    chain_rows = jnp.sum(jnp.where(mine, own_row, 0), axis=1, keepdims=True).astype(F32)
    shape = (tokens * HEADS, HEADS)
    mine = iota(shape, 1) == iota(shape, 0) % HEADS
    weight = jnp.sum(jnp.where(mine, chain_weight_ref[...], 0.0), axis=1, keepdims=True)
    biased_ref[...] = bias_ref[...] + jnp.where(chain_rows == chain_keys, weight, 0.0)
    rows = pick_ref.shape[0]
    counts = jnp.where(iota(table.shape, 1) < tokens, table, 0).astype(F32).astype(BF16)
    begin = jnp.zeros((1, TABLE), F32)
    size = jnp.zeros((1, TABLE), F32)
    for step in range(3):
        shape = (TABLE, TABLE)
        token = iota(shape, 1) - step * tokens
        here = (token >= 0) & (token < tokens)
        ahead = jnp.where(here & (iota(shape, 0) < token), 1.0, 0.0).astype(BF16)
        equal = jnp.where(here & (iota(shape, 0) == token), 1.0, 0.0).astype(BF16)
        at = owner(table.shape) == me + step - 1
        begin += jnp.sum(jnp.where(at, dot(counts, ahead), 0.0), axis=0, keepdims=True)
        size += jnp.sum(jnp.where(at, dot(counts, equal), 0.0), axis=0, keepdims=True)
        before = atoms_before(table, me + step - 1, tokens).astype(F32)
        begin += jnp.where(here[:1], before, 0.0)
    atom = (iota((rows, TABLE), 0) + me * rows).astype(F32)
    pick_ref[...] = jnp.where((atom >= begin) & (atom < begin + size), 1.0, 0.0).astype(BF16)
    gate_ref[...] = jax.nn.sigmoid(dot(normed, proj_ref[:, 3 * CS :]))
    copy.wait()


def attend_kernel(
    mine_ref, other_ref, query_ref, biased_ref, gate_ref, state_ref, wv_ref, out_ref, tokens_ref
):
    even = lax.rem(lax.axis_index("row"), 2) == 0
    tokens = state_ref.shape[0]
    chips = mine_ref.shape[0]
    mine, other = mine_ref[...], other_ref[...]
    first = jnp.where(even, mine, other)
    second = jnp.where(even, other, mine)
    normed = jnp.concatenate(
        [part[(c - chips // 2) % chips] for c in range(chips) for part in (first, second)], axis=0
    )
    scores = dot_nt(query_ref[...], normed) * (1.0 / math.sqrt(HDIM)) + biased_ref[...]
    weights = jnp.exp(scores - jnp.max(scores, axis=-1, keepdims=True))
    denom = jnp.sum(weights, axis=-1, keepdims=True)
    values = dot(normed, wv_ref[...]).astype(BF16)
    mixed = dot(weights.astype(BF16), values) / denom
    head = iota((HEADS, CS), 1) // HDIM == iota((HEADS, CS), 0)
    mixed = jnp.concatenate(
        [
            jnp.sum(
                jnp.where(head, mixed[t * HEADS : (t + 1) * HEADS], 0.0), axis=0, keepdims=True
            )
            for t in range(tokens)
        ],
        axis=0,
    )
    gated = (mixed * gate_ref[...]).astype(BF16)
    tokens_ref[...] = (state_ref[...] + dot(gated, out_ref[...])).astype(BF16)


def own_kernel(mid_ref, own_ref, pick_ref, weight_ref, back_ref, partial_ref, tokens_ref):
    own = own_ref[...]
    tokens_ref[...] = own
    back = dot(own, weight_ref[...]).astype(BF16)
    back_ref[...] = back
    count = back.shape[0]
    rest = jnp.zeros((TABLE - 2 * count, CA), BF16)
    spread = dot(pick_ref[...], jnp.concatenate([jnp.zeros_like(back), back, rest], axis=0))
    partial_ref[...] = mid_ref[...].astype(F32) + spread


def beside_kernel(partial_ref, core_ref, far_ref, pick_ref, weight_ref, atoms_ref):
    even = lax.rem(lax.axis_index("row"), 2) == 0
    core, far = core_ref[...], dot(far_ref[...], weight_ref[...]).astype(BF16)
    parts = [jnp.where(even, far, core), jnp.zeros_like(core), jnp.where(even, core, far)]
    rest = jnp.zeros((TABLE - 3 * core.shape[0], CA), BF16)
    spread = dot(pick_ref[...], jnp.concatenate([*parts, rest], axis=0))
    atoms_ref[...] = (partial_ref[...] + spread).astype(BF16)


def call(kernel, outs, *args, scratch=(), aliases=None):
    spec = pl.BlockSpec(memory_space=pltpu.VMEM)
    return pl.pallas_call(
        kernel,
        out_shape=outs,
        in_specs=[spec] * len(args),
        out_specs=jax.tree.map(lambda _: spec, outs),
        scratch_shapes=list(scratch),
        input_output_aliases=aliases or {},
        compiler_params=pltpu.CompilerParams(vmem_limit_bytes=VMEM_LIMIT),
        cost_estimate=pl.CostEstimate(flops=COST, bytes_accessed=COST // 200, transcendentals=0),
    )(*args)


def shape_of(shape, dtype):
    return jax.ShapeDtypeStruct(shape, dtype)


def shards(
    atom_feat,
    window_start,
    atom_count,
    residue_type,
    chain_id,
    token_single,
    pair,
    atom_gain,
    atom_qkv,
    atom_out,
    pool_weight,
    restype_table,
    token_gain,
    token_proj,
    token_out,
    pair_gain,
    pair_bias_weight,
    chain_weight,
    back_weight,
):
    n = lax.axis_size("row")
    rows, tokens, extent = atom_feat.shape[0], token_single.shape[0], pair.shape[1]
    cores = [(i, i ^ 1) for i in range(n)]
    far = [(i, i + 1) for i in range(1, n - 1, 2)] + [(i + 1, i) for i in range(1, n - 1, 2)]
    chips = n // 2
    same_core = [[2 * ((c + chips // 2) % chips) + core for c in range(chips)] for core in range(2)]
    backwards = [list(reversed(range(n)))]

    feat_far = lax.ppermute(atom_feat, "row", far)
    feat_core = lax.ppermute(atom_feat, "row", cores)
    table = call(
        table_kernel,
        shape_of((n, 1, TABLE), jnp.int32),
        call(first_kernel, shape_of((8, TABLE), jnp.int32)),
        atom_count[None],
        chain_id[None],
        residue_type[None],
        window_start[None],
    )
    table = lax.all_to_all(table, "row", 0, 0, tiled=True, axis_index_groups=backwards).reshape(n, TABLE)

    bias = call(
        pair_kernel, shape_of((tokens * HEADS, extent), F32), pair, pair_gain, pair_bias_weight.T
    )
    values, scores, mid, lifted = call(
        functools.partial(atom_kernel, n),
        (
            shape_of((rows + 2 * HALF, CA), BF16),
            shape_of((2, AHEADS * REACH, 2 * HALF), F32),
            shape_of((rows, CA), BF16),
            shape_of((rows, CS), BF16),
        ),
        atom_feat,
        feat_core,
        feat_far,
        window_start[None],
        atom_gain,
        atom_qkv,
        atom_out,
        pool_weight,
        bias,
    )
    state, normed = call(
        functools.partial(state_kernel, n),
        (shape_of((tokens, CS), F32), shape_of((n // 2, tokens, CS), BF16)),
        values,
        scores,
        lifted,
        feat_core,
        feat_far,
        table,
        token_single,
        atom_out,
        pool_weight,
        restype_table,
        token_gain,
    )
    mine = lax.all_to_all(normed, "row", 0, 0, tiled=True, axis_index_groups=same_core)
    query, gate, biased, pick, wv = call(
        query_kernel,
        (
            shape_of((tokens * HEADS, CS), BF16),
            shape_of((tokens, CS), F32),
            shape_of((tokens * HEADS, extent), F32),
            shape_of((rows, TABLE), BF16),
            shape_of((CS, CS), BF16),
        ),
        normed,
        table,
        bias,
        chain_weight,
        token_proj,
        scratch=(pltpu.SemaphoreType.DMA,),
        aliases={2: 2},
    )
    mine, query = lax.optimization_barrier((mine, query))
    other = lax.ppermute(mine, "row", cores)
    updated = call(
        attend_kernel,
        shape_of((tokens, CS), BF16),
        mine,
        other,
        query,
        biased,
        gate,
        state,
        wv,
        token_out,
    )
    tokens_far = lax.ppermute(updated, "row", far)
    back, partial, tokens_out = call(
        own_kernel,
        (shape_of((tokens, CA), BF16), shape_of((rows, CA), F32), shape_of((tokens, CS), BF16)),
        mid,
        updated,
        pick,
        back_weight,
    )
    back_core = lax.ppermute(back, "row", cores)
    atoms_out = call(
        beside_kernel,
        shape_of((rows, CA), BF16),
        partial,
        back_core,
        tokens_far,
        pick,
        back_weight,
    )
    return (atoms_out, tokens_out)


def solution(mesh):
    split = P(("groups", "row"), None)
    line = P(("groups", "row"))
    return jax.shard_map(
        shards,
        mesh=mesh,
        in_specs=(split, line, line, line, line, split, P(("groups", "row"), None, None))
        + (P(),) * 12,
        out_specs=(split, split),
        check_vma=False,
    )
```
